256 devices in a mesh: heads: 4 (over x_lo, core), blk: 64 (over x_hi, y, z).
Axes of the slice: x: 4 (x_hi: 2, x_lo: 2; x = x_hi * 2 + x_lo), y: 4, z: 8, core: 2. Of those that a mesh axis runs over, the one named last changes fastest.
Arguments:
- queries: bfloat16 [512, 128, 576], P('blk', 'heads'), may hold values from -12 to 12
- prefix_latent: bfloat16 [16384, 576], P('blk'), may hold values from -6 to 6
- suffix_latent: bfloat16 [512, 64, 576], P('blk'), may hold values from -10 to 10
- suffix_len: int32 [512], P('blk'), may hold values from 1 to 64, 16384 in all
- prefix_blocks: int32 [64], replicated, may hold values from 0 to 63, as said below
- caption_reach: int32 [512], P('blk'), may hold values from 1 to 64, as said below
- w_uv: bfloat16 [128, 512, 128], P('heads'), may hold values from -0.25 to 0.25
- w_out: bfloat16 [16384, 5120], P('heads', 'blk'), may hold values from -0.046875 to 0.046875
Outputs:
- mixed: bfloat16 [512, 5120], P('heads', 'blk')
The draws below stay inside these ranges and needn't reach their ends.
Inputs may be any that keep to these rules, and one draw needn't show every extreme that they name: `suffix_len`: some caption has exactly 64 live suffix tokens. `prefix_blocks`: each of 0 to 63 once. `caption_reach`: some caption sees all 64 blocks and some only block 0.
All inputs are finite; a program needn't handle non-finite values. No bound on the sum of `suffix_len` on one device may be relied on, other than what follows from the above.
Results may differ from the reference program's by a relative error of at most 0.02.
Values may be sent and summed in bfloat16 or wider, within the bound.
A program may use at most 128 MiB of HBM per device.

```python
import math
import jax
import jax.numpy as jnp
import numpy as np
from jax import lax

HEADS = 128
LAT = 512
VD = 128
DM = 5120
P_DEV = 256
S_MAX = 64
KW = 576
BLOCKS = 64
CAPTIONS = 512
PREFIX = 16384


def block_order(key):
    return jax.random.permutation(jax.random.fold_in(key, 11), BLOCKS).astype(jnp.int32)


def prefix_rows(key):
    base = jax.random.fold_in(key, 12)
    normal_part = jax.random.truncated_normal(jax.random.fold_in(base, 1), -5.0, 5.0, (PREFIX, KW), jnp.float32)
    return normal_part


def draw_prefix_blocks(key, part):
    order = block_order(key)
    return order


def draw_prefix_latent(key, part):
    return prefix_rows(key).astype(jnp.bfloat16)


def draw_queries(key, part):
    key = jax.random.fold_in(key, 5)
    return (jax.random.truncated_normal(jax.random.fold_in(key, 1), -6.0, 6.0, (CAPTIONS, HEADS, KW), jnp.float32) * 1.3).astype(jnp.bfloat16)


def draw_caption_reach(key, part):
    key = jax.random.fold_in(key, 7)
    reach = jax.random.randint(key, (CAPTIONS,), 1, BLOCKS + 1).astype(jnp.int32)
    return reach.at[0].set(BLOCKS).at[1].set(1)


def block_scale(stream_key, shape, shards, smallest, high):
    def one(dim, shards_of):
        heights = jax.random.uniform(jax.random.fold_in(jax.random.fold_in(stream_key, 6), dim), (shards_of,), jnp.float32, smallest / len(shards), high / len(shards))
        return jnp.repeat(jnp.exp(heights), shape[dim] // shards_of).reshape((-1,) + (1,) * (len(shape) - dim - 1))

    level = one(*shards[0])
    for cut in shards[1:]:
        level = level * one(*cut)
    return level


def profile(number_of, total, most, skew):
    weights = [(1 << 20) // math.isqrt(grade ** skew) + 1 for grade in range(2, number_of + 1)]
    spare, given = total - most - (number_of - 1), [1] * (number_of - 1)
    while spare > 0:
        movable = [i for i in range(number_of - 1) if given[i] < most]
        mass, remaining = sum([weights[i] for i in movable]), spare
        for i in movable:
            more = min(most - given[i], max(1, remaining * weights[i] // mass), spare)
            given[i] = given[i] + more
            spare = spare - more
    return np.array([most] + given)


def uneven_parts(key, number_of, total, most, skew):
    if number_of == 2:
        one = jax.random.randint(key, (), max(1, total - most), min(most, total - 1) + 1)
        return jnp.stack([one, total - one])
    lengths = jnp.asarray(profile(number_of, total, most, skew), jnp.int32)
    pairs = (number_of - 1) // 2
    donor, taker = lengths[1:1 + 2 * pairs:2], lengths[2:2 + 2 * pairs:2]
    slack = jnp.minimum(donor - 1, most - taker)
    moved = jax.random.randint(jax.random.fold_in(key, 1), (pairs,), 0, 1 << 20) % (slack + 1)
    lengths = lengths.at[1:1 + 2 * pairs:2].set(donor - moved).at[2:2 + 2 * pairs:2].set(taker + moved)
    return lengths[jax.random.permutation(jax.random.fold_in(key, 2), number_of)]


def centred(own_key, extent, width, bound, pieces=(), kind=jnp.bfloat16):
    loudness = block_scale(own_key, extent, pieces, -0.22, 0.18) if pieces else 1.0
    entries = jax.random.normal(own_key, extent, jnp.float32) * width * loudness
    return jnp.minimum(jnp.maximum(entries, -bound), bound).astype(kind)


def setup_inputs(seed: int = 0) -> dict:
    arg_keys = jax.random.split(jax.random.key(seed), 9)
    queries = draw_queries(jax.random.fold_in(arg_keys[8], 71), 0)
    prefix_latent = draw_prefix_latent(jax.random.fold_in(arg_keys[8], 71), 0)
    suffix_latent = centred(arg_keys[2], (CAPTIONS, S_MAX, KW), 2.0, 10.0, ((0, 64),))
    suffix_len = uneven_parts(arg_keys[3], CAPTIONS, CAPTIONS * S_MAX // 2, S_MAX, 1).astype(jnp.int32)
    prefix_blocks = draw_prefix_blocks(jax.random.fold_in(arg_keys[8], 71), 0)
    caption_reach = draw_caption_reach(jax.random.fold_in(arg_keys[8], 71), 0)
    w_uv = centred(arg_keys[6], (HEADS, LAT, VD), LAT ** -0.5, 0.25, ((0, 4),))
    w_out = centred(arg_keys[7], (HEADS * VD, DM), (HEADS * VD) ** -0.5, 0.046875, ((0, 4), (1, 64)))
    return {"queries": queries, "prefix_latent": prefix_latent, "suffix_latent": suffix_latent, "suffix_len": suffix_len, "prefix_blocks": prefix_blocks, "caption_reach": caption_reach, "w_uv": w_uv, "w_out": w_out}


SCALE = 192.0 ** -0.5
NEG = -1.0e30


def reference(queries, prefix_latent, suffix_latent, suffix_len, prefix_blocks, caption_reach, w_uv, w_out):
    row_block = jnp.repeat(prefix_blocks, P_DEV, total_repeat_length=PREFIX)
    content = prefix_latent[:, :LAT]
    positions = jnp.arange(S_MAX, dtype=jnp.int32)

    def one_caption(item):
        query, suffix, length, reach = item
        scores = jnp.dot(query, prefix_latent.T, preferred_element_type=jnp.float32) * SCALE
        seen = (row_block < reach)[None, :]
        scores = jnp.where(seen, scores, NEG)
        tail = jnp.dot(query, suffix.T, preferred_element_type=jnp.float32) * SCALE
        live = (positions < length)[None, :]
        tail = jnp.where(live, tail, NEG)
        top = jnp.maximum(jnp.max(scores, axis=1), jnp.max(tail, axis=1))
        weights = jnp.where(seen, jnp.exp(scores - top[:, None]), jnp.float32(0.0))
        tail_weights = jnp.where(live, jnp.exp(tail - top[:, None]), jnp.float32(0.0))
        total = jnp.sum(weights, axis=1) + jnp.sum(tail_weights, axis=1)
        summed = jnp.dot(weights.astype(jnp.bfloat16), content, preferred_element_type=jnp.float32)
        summed = summed + jnp.dot(tail_weights.astype(jnp.bfloat16), suffix[:, :LAT], preferred_element_type=jnp.float32)
        return (summed / total[:, None]).astype(jnp.bfloat16)

    attn = lax.map(one_caption, (queries, suffix_latent, suffix_len, caption_reach))
    head_value = jnp.einsum("chl,hlv->chv", attn.astype(jnp.float32), w_uv.astype(jnp.float32)).astype(jnp.bfloat16)
    flat = head_value.reshape(CAPTIONS, HEADS * VD)
    return jnp.dot(flat, w_out, preferred_element_type=jnp.float32).astype(jnp.bfloat16)
```

```python
import jax
import jax.numpy as jnp
from jax import lax
from jax.experimental import pallas as pl
from jax.experimental.pallas import tpu as pltpu
from jax.sharding import PartitionSpec as P

C2 = (192.0 ** -0.5) * 1.4426950408889634
NEG = -1.0e30
NT = (((1,), (1,)), ((), ()))
NN = (((1,), (0,)), ((), ()))
F32 = jnp.float32
BF16 = jnp.bfloat16
MESH = pl.DeviceIdType.MESH


def dot(a, b, dims):
    return lax.dot_general(a, b, dims, preferred_element_type=F32)


def kernel(
    q_hbm, k_hbm, s_hbm, uv_hbm, w_hbm, len_ref, blocks_ref, reach_ref, out_ref,
    q_in, k_in, s_in, uv, w_in,
    qbuf, kbuf, acc, m_ref, l_ref,
    w_t, wbuf, hv_send, lse_full, lse_send, hv_recv, lse_recv,
    units, hv_all, out_send, rs,
    in_sem, kz_s, kz_r, kx_s, kx_r, kc_s, kc_r, q_s, q_r, w_s, w_r,
    a_s, a_r, h_s, h_r, rs_s, rs_r,
):
    hd = lax.axis_index("heads")
    b = lax.axis_index("blk")
    p, c = hd // 2, hd % 2
    xh, y, z = b // 32, (b // 8) % 4, b % 8

    def dev(xh_=None, y_=None, z_=None, p_=None, c_=None):
        xx = xh if xh_ is None else xh_
        yy = y if y_ is None else y_
        zz = z if z_ is None else z_
        pp = p if p_ is None else p_
        cc = c if c_ is None else c_
        return (pp * 2 + cc, xx * 32 + yy * 8 + zz)

    zp, zm = dev(z_=(z + 1) % 8), dev(z_=(z + 7) % 8)
    same_x, other_x = dev(p_=1 - p), dev(xh_=1 - xh, p_=1 - p)
    sib, across = dev(c_=1 - c), dev(xh_=1 - xh)

    def peer(d, dh):
        return dev(
            y_=(y + 4 - d) % 4,
            p_=p if dh // 2 == 0 else 1 - p,
            c_=c if dh % 2 == 0 else 1 - c,
        )

    local = []
    for n, (src, dst) in enumerate(
        ((q_hbm, q_in), (k_hbm, k_in), (s_hbm, s_in), (w_hbm, w_in), (uv_hbm, uv))
    ):
        copy = pltpu.make_async_copy(src, dst, in_sem.at[n])
        copy.start()
        local.append(copy)

    partners = [zp, zm, other_x, across]
    partners += [peer(d, dh) for d in range(4) for dh in range(4) if d or dh]
    barrier = pltpu.get_barrier_semaphore()
    for who in partners:
        pl.semaphore_signal(barrier, inc=1, device_id=who, device_id_type=MESH)

    sent = []

    def send(src, dst, ssem, rsem, who):
        copy = pltpu.make_async_remote_copy(
            src_ref=src, dst_ref=dst, send_sem=ssem, recv_sem=rsem,
            device_id=who, device_id_type=MESH,
        )
        copy.start()
        sent.append(copy)
        return copy

    lanes = lax.broadcasted_iota(jnp.int32, (1, 64), 1)
    local[1].wait()
    own = (lanes == blocks_ref[b]).astype(F32)
    kbuf[0, 0:256, 0:576] = k_in[...]
    kbuf[0, 0:256, 576:640] = jnp.broadcast_to(own, (256, 64)).astype(BF16)
    local[0].wait()
    qbuf[0, :, 0:576] = q_in[...]
    for i in range(8):
        seen = jnp.where(lanes >= reach_ref[i], F32(NEG), F32(0.0))
        qbuf[0, 32 * i : 32 * i + 32, 576:640] = jnp.broadcast_to(seen, (32, 64)).astype(BF16)

    pl.semaphore_wait(barrier, len(partners))

    quarter = pl.ds(pl.multiple_of(128 * p + 64 * c, 64), 64)
    quarter_x = pl.ds(pl.multiple_of(128 * (1 - p) + 64 * c, 64), 64)
    ox = [
        send(kbuf.at[0, quarter_x], kbuf.at[0, 256:320], kx_s.at[0, 0], kx_r.at[0, 0], other_x)
    ]
    kz = {}

    def ring(buf, r, xb, src, dst, s_sem, r_sem, table):
        forward = r <= 3 or (r == 4 and xb == 0)
        table[r, xb] = send(src, dst, s_sem.at[r, xb], r_sem.at[r, xb], zp if forward else zm)

    def k_rows(r, xb):
        return kbuf.at[r, 64 * xb : 64 * xb + 64]

    for r in (1, 7):
        ring(kbuf, r, 0, kbuf.at[0, quarter], k_rows(r, 0), kz_s, kz_r, kz)
    qp = send(qbuf.at[0], qbuf.at[1], q_s.at[0], q_r.at[0], dev(y_=(y + 1) % 4))
    qm = send(qbuf.at[0], qbuf.at[3], q_s.at[1], q_r.at[1], dev(y_=(y + 3) % 4))
    ox.append(
        send(kbuf.at[0, quarter], kbuf.at[0, 320:384], kx_s.at[0, 1], kx_r.at[0, 1], other_x)
    )
    local[2].wait()
    m_ref[...] = jnp.full_like(m_ref, NEG)
    l_ref[...] = jnp.zeros_like(l_ref)
    acc[...] = jnp.zeros_like(acc)
    ox[0].wait_recv()
    for r in (1, 7):
        ring(kbuf, r, 1, kbuf.at[0, 256:320], k_rows(r, 1), kz_s, kz_r, kz)

    spot = lax.broadcasted_iota(jnp.int32, (1, 64), 1)

    def suffix(i, carry):
        rows = pl.ds(pl.multiple_of(i * 32, 32), 32)
        toks = pl.ds(pl.multiple_of(i * 64, 64), 64)
        sc = dot(qbuf[0, rows, 0:576], s_in[toks, :], NT) * C2
        sc = jnp.where(spot < len_ref[i], sc, F32(NEG))
        top = jnp.max(sc, axis=1, keepdims=True)
        weight = jnp.exp2(sc - top)
        m_ref[rows, :] = jnp.broadcast_to(top, (32, 128))
        l_ref[rows, :] = jnp.broadcast_to(jnp.sum(weight, axis=1, keepdims=True), (32, 128))
        start = dot(weight.astype(BF16), s_in[toks, 0:512], NN)
        for j in range(4):
            acc[j, rows, :] = start[:, 128 * j : 128 * j + 128]
        return carry

    lax.fori_loop(0, 8, suffix, 0)

    ox[1].wait_recv()
    sib0 = send(kbuf.at[0, 256:384], kbuf.at[0, 384:512], kc_s.at[0, 0], kc_r.at[0, 0], sib)

    def score(s, r):
        return dot(qbuf[s], kbuf[r], NT)

    def fold(s, r, sc):
        rows = pl.ds(s * 256, 256)
        before = m_ref[rows, :]
        after = jnp.maximum(before, jnp.max(sc, axis=1, keepdims=True) * C2)
        shrink = jnp.exp2(before - after)
        weight = jnp.exp2(sc * C2 - after[:, :1])
        l_ref[rows, :] = l_ref[rows, :] * shrink + jnp.sum(weight, axis=1, keepdims=True)
        m_ref[rows, :] = after
        more = dot(weight.astype(BF16), kbuf[r, :, 0:512], NN)
        for j in range(4):
            acc[j, rows, :] = acc[j, rows, :] * shrink + more[:, 128 * j : 128 * j + 128]

    def attend(todo):
        now = score(*todo[0])
        for n, (s, r) in enumerate(todo):
            later = score(*todo[n + 1]) if n + 1 < len(todo) else None
            fold(s, r, now)
            now = later

    kx, kc = {}, {}

    def from_z(r):
        for xb in (0, 1):
            kz[r, xb].wait_recv()
            if r in (1, 2):
                ring(kbuf, r + 1, xb, k_rows(r, xb), k_rows(r + 1, xb), kz_s, kz_r, kz)
            elif r in (7, 6):
                ring(kbuf, r - 1, xb, k_rows(r, xb), k_rows(r - 1, xb), kz_s, kz_r, kz)
            elif (r, xb) in ((3, 0), (5, 1)):
                ring(kbuf, 4, xb, k_rows(r, xb), k_rows(4, xb), kz_s, kz_r, kz)
            if xb == 0:
                kx[r] = (
                    send(kbuf.at[r, 0:64], kbuf.at[r, 128:192], kx_s.at[r, 0], kx_r.at[r, 0], same_x),
                    send(kbuf.at[r, 0:64], kbuf.at[r, 192:256], kx_s.at[r, 1], kx_r.at[r, 1], other_x),
                )
        kc[r] = [send(kbuf.at[r, 0:128], kbuf.at[r, 256:384], kc_s.at[r, 0], kc_r.at[r, 0], sib)]

    def from_x(r):
        for copy in kx[r]:
            copy.wait_recv()
        kc[r].append(
            send(kbuf.at[r, 128:256], kbuf.at[r, 384:512], kc_s.at[r, 1], kc_r.at[r, 1], sib)
        )

    def ready(r):
        for copy in kc[r]:
            copy.wait_recv()

    local[3].wait()

    def turn(i, carry):
        w_t[i] = w_in[pl.ds(pl.multiple_of(i * 1024, 1024), 1024), :].T
        return carry

    lax.fori_loop(0, 4, turn, 0)
    wbuf[0:80, :] = w_t[y]

    sib0.wait_recv()
    attend([(0, 0)])
    from_z(1)
    from_z(7)
    from_x(1)
    from_x(7)
    ready(1)
    ready(7)
    attend([(0, 1), (0, 7)])
    qp.wait_recv()
    qfp = send(qbuf.at[1, 0:128], qbuf.at[2, 0:128], q_s.at[2], q_r.at[2], dev(y_=(y + 1) % 4))
    qm.wait_recv()
    qfm = send(qbuf.at[3, 128:256], qbuf.at[2, 128:256], q_s.at[3], q_r.at[3], dev(y_=(y + 3) % 4))
    ws = [
        send(w_t.at[(y + d) % 4], wbuf.at[80 * d : 80 * d + 80], w_s.at[d], w_r.at[d], dev(y_=(y + d) % 4))
        for d in (1, 3, 2)
    ]
    from_z(2)
    from_z(6)
    attend([(1, 0), (3, 0), (1, 1), (3, 1)])
    from_x(2)
    from_x(6)
    attend([(1, 7), (3, 7)])
    ready(2)
    ready(6)
    from_z(3)
    from_z(5)
    attend([(0, 2), (1, 2), (3, 2)])
    from_x(3)
    from_x(5)
    from_z(4)
    attend([(0, 6), (1, 6), (3, 6)])
    qfp.wait_recv()
    qfm.wait_recv()
    from_x(4)
    attend([(2, 0), (2, 1), (2, 7), (2, 2), (2, 6)])
    ready(3)
    ready(5)
    ready(4)

    def last(i, carry):
        r = 3 + i
        attend([(0, r), (1, r), (2, r), (3, r)])
        return carry

    lax.fori_loop(0, 3, last, 0)

    local[4].wait()

    def up(h, carry):
        parts, logs = [], []
        for a in range(4):
            s = (y + 4 - a) % 4
            rows = pl.ds(s * 256 + h, 8, stride=32)
            tot = l_ref[rows, :]
            inv = 1.0 / tot
            parts.append(jnp.concatenate([acc[j, rows, :] * inv for j in range(4)], axis=1))
            logs.append(m_ref[rows, :] + jnp.log2(tot))
        attn = jnp.concatenate(parts, axis=0).astype(BF16)
        value = dot(attn, uv[h], NN)
        place = pl.ds(pl.multiple_of((h % 8) * 32, 32), 32)
        hv_send[h // 8, place, :] = value.astype(BF16)
        lse_full[h // 8, place, :] = jnp.concatenate(logs, axis=0)
        return carry

    lax.fori_loop(0, 32, up, 0)

    def flat(i, carry):
        lse_send[i] = lse_full[i].T[0:8, :]
        return carry

    lax.fori_loop(0, 4, flat, 0)

    heads_out = []
    for d in (2, 1, 3):
        to = (y + d) % 4
        heads_out.append(
            (
                send(hv_send.at[to], hv_recv.at[d], a_s.at[d, 0], a_r.at[d, 0], dev(y_=to)),
                send(lse_send.at[to], lse_recv.at[d], a_s.at[d, 1], a_r.at[d, 1], dev(y_=to)),
            )
        )
    for pair in heads_out:
        for copy in pair:
            copy.wait_recv()
    logs = [lse_send[y]] + [lse_recv[d] for d in (1, 2, 3)]
    best = jnp.maximum(jnp.maximum(logs[0], logs[1]), jnp.maximum(logs[2], logs[3]))
    part = [jnp.exp2(x - best) for x in logs]
    norm = 1.0 / (part[0] + part[1] + part[2] + part[3])
    total = None
    for d in range(4):
        share = jnp.concatenate([part[d] * norm] * 16, axis=0).T
        term = share * (hv_send[y] if d == 0 else hv_recv[d]).astype(F32)
        total = term if d == 0 else total + term
    total = total.astype(BF16)
    for h in range(8):
        units[0, 0, :, 128 * h : 128 * h + 128] = total[32 * h : 32 * h + 32, :]

    hz = {}
    hx = send(units.at[0, 0], units.at[0, 1], h_s.at[0, 0], h_r.at[0, 0], across)
    for r in (1, 7):
        ring(units, r, 0, units.at[0, 0], units.at[r, 0], h_s, h_r, hz)

    def place_unit(r, xb):
        base = (xh if xb == 0 else 1 - xh) * 256 + ((z + 8 - r) % 8) * 8
        unit = units[r, xb].astype(F32)
        for a in range(4):
            hv_all[pl.ds(pl.multiple_of(base + 64 * a, 8), 8), :] = unit[8 * a : 8 * a + 8, :]

    place_unit(0, 0)
    hx.wait_recv()
    for r in (1, 7):
        ring(units, r, 1, units.at[0, 1], units.at[r, 1], h_s, h_r, hz)
    place_unit(0, 1)
    for r in (1, 7, 2, 6, 3, 5, 4):
        for xb in (0, 1):
            hz[r, xb].wait_recv()
            if r in (1, 2):
                ring(units, r + 1, xb, units.at[r, xb], units.at[r + 1, xb], h_s, h_r, hz)
            elif r in (7, 6):
                ring(units, r - 1, xb, units.at[r, xb], units.at[r - 1, xb], h_s, h_r, hz)
            elif (r, xb) in ((3, 0), (5, 1)):
                ring(units, 4, xb, units.at[r, xb], units.at[4, xb], h_s, h_r, hz)
        for xb in (0, 1):
            place_unit(r, xb)

    for copy in ws:
        copy.wait_recv()
    for h in range(4):
        cols = dot(wbuf[...], hv_all[128 * h : 128 * h + 128, :].astype(BF16), NT)
        out_send[h] = cols.astype(BF16)
    back = []
    for d in (2, 1, 3, 0):
        for dh in range(4):
            if d or dh:
                who = peer(d, dh)
                back.append(
                    send(
                        out_send.at[who[0], 80 * d : 80 * d + 80], rs.at[4 * d + dh],
                        rs_s.at[4 * d + dh], rs_r.at[4 * d + dh], who,
                    )
                )
    result = out_send[hd, 0:80, :].astype(F32)
    for copy in back:
        copy.wait_recv()
    for n in range(1, 16):
        result = result + rs[n].astype(F32)
    out_ref[...] = result.T.astype(BF16)
    for copy in sent:
        copy.wait_send()


def per_device(
    queries, prefix_latent, suffix_latent, suffix_len, prefix_blocks, caption_reach, w_uv, w_out
):
    dma = pltpu.SemaphoreType.DMA
    return pl.pallas_call(
        kernel,
        out_shape=jax.ShapeDtypeStruct((128, 80), BF16),
        in_specs=[pl.BlockSpec(memory_space=pl.ANY)] * 5
        + [pl.BlockSpec(memory_space=pltpu.SMEM)] * 3,
        out_specs=pl.BlockSpec(memory_space=pltpu.VMEM),
        scratch_shapes=[
            pltpu.VMEM((256, 576), BF16),
            pltpu.VMEM((256, 576), BF16),
            pltpu.VMEM((512, 576), BF16),
            pltpu.VMEM((32, 512, 128), BF16),
            pltpu.VMEM((4096, 80), BF16),
            pltpu.VMEM((4, 256, 640), BF16),
            pltpu.VMEM((8, 512, 640), BF16),
            pltpu.VMEM((4, 1024, 128), F32),
            pltpu.VMEM((1024, 128), F32),
            pltpu.VMEM((1024, 128), F32),
            pltpu.VMEM((4, 80, 1024), BF16),
            pltpu.VMEM((320, 1024), BF16),
            pltpu.VMEM((4, 256, 128), BF16),
            pltpu.VMEM((4, 256, 128), F32),
            pltpu.VMEM((4, 8, 256), F32),
            pltpu.VMEM((4, 256, 128), BF16),
            pltpu.VMEM((4, 8, 256), F32),
            pltpu.VMEM((8, 2, 32, 1024), BF16),
            pltpu.VMEM((512, 1024), F32),
            pltpu.VMEM((4, 320, 128), BF16),
            pltpu.VMEM((16, 80, 128), BF16),
            dma((5,)),
            dma((8, 2)), dma((8, 2)),
            dma((8, 2)), dma((8, 2)),
            dma((8, 2)), dma((8, 2)),
            dma((4,)), dma((4,)),
            dma((4,)), dma((4,)),
            dma((4, 2)), dma((4, 2)),
            dma((8, 2)), dma((8, 2)),
            dma((16,)), dma((16,)),
        ],
        compiler_params=pltpu.CompilerParams(
            collective_id=0, has_side_effects=True, vmem_limit_bytes=56 * 2**20
        ),
    )(
        queries.reshape(256, 576),
        prefix_latent,
        suffix_latent.reshape(512, 576),
        w_uv,
        w_out,
        suffix_len,
        prefix_blocks,
        caption_reach,
    )


def solution(mesh):
    placed = (
        P("blk", "heads", None),
        P("blk", None),
        P("blk", None, None),
        P("blk"),
        P(),
        P("blk"),
        P("heads", None, None),
        P("heads", "blk"),
    )
    return jax.shard_map(
        per_device, mesh=mesh, in_specs=placed, out_specs=P("heads", "blk"), check_vma=False
    )
```

```python
import jax
import jax.numpy as jnp
from jax import lax
from jax.experimental import pallas as pl
from jax.experimental.pallas import tpu as pltpu
from jax.sharding import PartitionSpec as P

C2 = (192.0 ** -0.5) * 1.4426950408889634
NEG = -1.0e30
NT = (((1,), (1,)), ((), ()))
NN = (((1,), (0,)), ((), ()))
F32 = jnp.float32
BF16 = jnp.bfloat16
MESH = pl.DeviceIdType.MESH


def dot(a, b, dims):
    return lax.dot_general(a, b, dims, preferred_element_type=F32)


def kernel(
    q_hbm, k_hbm, s_hbm, uv_hbm, w_hbm, len_ref, blocks_ref, reach_ref, out_ref,
    q_in, k_in, s_in, uv, w_in,
    qbuf, kbuf, acc, m_ref, l_ref,
    wbuf, hv_send, lse_full, lse_send, hv_recv, lse_recv,
    units, hv_all, out_send, rs,
    in_sem, kz_s, kz_r, kx_s, kx_r, kc_s, kc_r, q_s, q_r, w_s, w_r,
    a_s, a_r, h_s, h_r, rs_s, rs_r,
):
    hd = lax.axis_index("heads")
    b = lax.axis_index("blk")
    p, c = hd // 2, hd % 2
    xh, y, z = b // 32, (b // 8) % 4, b % 8

    def dev(xh_=None, y_=None, z_=None, p_=None, c_=None):
        xx = xh if xh_ is None else xh_
        yy = y if y_ is None else y_
        zz = z if z_ is None else z_
        pp = p if p_ is None else p_
        cc = c if c_ is None else c_
        return (pp * 2 + cc, xx * 32 + yy * 8 + zz)

    zp, zm = dev(z_=(z + 1) % 8), dev(z_=(z + 7) % 8)
    same_x, other_x = dev(p_=1 - p), dev(xh_=1 - xh, p_=1 - p)
    sib, across = dev(c_=1 - c), dev(xh_=1 - xh)

    def peer(d, dh):
        return dev(
            y_=(y + 4 - d) % 4,
            p_=p if dh // 2 == 0 else 1 - p,
            c_=c if dh % 2 == 0 else 1 - c,
        )

    local = []
    for n, (src, dst) in enumerate(
        ((q_hbm, q_in), (k_hbm, k_in), (s_hbm, s_in), (w_hbm, w_in), (uv_hbm, uv))
    ):
        copy = pltpu.make_async_copy(src, dst, in_sem.at[n])
        copy.start()
        local.append(copy)

    partners = [zp, zm, other_x, across]
    partners += [peer(d, dh) for d in range(4) for dh in range(4) if d or dh]
    barrier = pltpu.get_barrier_semaphore()
    for who in partners:
        pl.semaphore_signal(barrier, inc=1, device_id=who, device_id_type=MESH)

    sent = []

    def send(src, dst, ssem, rsem, who):
        copy = pltpu.make_async_remote_copy(
            src_ref=src, dst_ref=dst, send_sem=ssem, recv_sem=rsem,
            device_id=who, device_id_type=MESH,
        )
        copy.start()
        sent.append(copy)
        return copy

    m_ref[...] = jnp.full_like(m_ref, NEG)
    l_ref[...] = jnp.zeros_like(l_ref)
    acc[...] = jnp.zeros_like(acc)
    lanes = lax.broadcasted_iota(jnp.int32, (1, 64), 1)
    local[1].wait()
    own = (lanes == blocks_ref[b]).astype(F32)
    turn = lax.broadcasted_iota(jnp.int32, (256, 256), 0) == lax.broadcasted_iota(
        jnp.int32, (256, 256), 1
    )
    kbuf[0, 0:256, 0:576] = dot(turn.astype(F32).astype(BF16), k_in[...], NT).astype(BF16)
    kbuf[0, 0:256, 576:640] = jnp.broadcast_to(own, (256, 64)).astype(BF16)
    local[0].wait()
    qbuf[0, :, 0:576] = q_in[...]
    for i in range(8):
        seen = jnp.where(lanes >= reach_ref[i], F32(NEG), F32(0.0))
        qbuf[0, 32 * i : 32 * i + 32, 576:640] = jnp.broadcast_to(seen, (32, 64)).astype(BF16)

    pl.semaphore_wait(barrier, len(partners))

    quarter = pl.ds(pl.multiple_of(128 * p + 64 * c, 64), 64)
    quarter_x = pl.ds(pl.multiple_of(128 * (1 - p) + 64 * c, 64), 64)
    yp, ym = dev(y_=(y + 1) % 4), dev(y_=(y + 3) % 4)
    kz = {}

    def ring(r, xb, src, dst, s_sem, r_sem, table):
        forward = r <= 3 or (r == 4 and xb == 0)
        table[r, xb] = send(src, dst, s_sem.at[r, xb], r_sem.at[r, xb], zp if forward else zm)

    def k_rows(r, xb):
        return kbuf.at[r, 64 * xb : 64 * xb + 64]

    def q_send(n, s_from, s_to, half, who):
        rows = slice(128 * half, 128 * half + 128)
        return send(qbuf.at[s_from, rows], qbuf.at[s_to, rows], q_s.at[n], q_r.at[n], who)

    ox = [
        send(kbuf.at[0, quarter_x], kbuf.at[0, 256:320], kx_s.at[0, 0], kx_r.at[0, 0], other_x)
    ]
    for r in (1, 7):
        ring(r, 0, kbuf.at[0, quarter], k_rows(r, 0), kz_s, kz_r, kz)
    qp = [q_send(0, 0, 1, 0, yp)]
    qm = [q_send(1, 0, 3, 1, ym)]
    ox.append(
        send(kbuf.at[0, quarter], kbuf.at[0, 320:384], kx_s.at[0, 1], kx_r.at[0, 1], other_x)
    )
    qp.append(q_send(2, 0, 1, 1, yp))
    qm.append(q_send(3, 0, 3, 0, ym))

    local[2].wait()

    def suffix(i, carry):
        for n in range(4):
            rows = pl.ds(pl.multiple_of(i * 128 + n * 32, 32), 32)
            toks = pl.ds(pl.multiple_of(i * 256 + n * 64, 64), 64)
            sc = dot(qbuf[0, rows, 0:576], s_in[toks, :], NT) * C2
            sc = jnp.where(lanes < len_ref[4 * i + n], sc, F32(NEG))
            top = jnp.max(sc, axis=1, keepdims=True)
            weight = jnp.exp2(sc - top)
            m_ref[rows, :] = jnp.broadcast_to(top, (32, 128))
            l_ref[rows, :] = jnp.broadcast_to(jnp.sum(weight, axis=1, keepdims=True), (32, 128))
            start = dot(weight.astype(BF16), s_in[toks, 0:512], NN)
            for j in range(4):
                acc[j, rows, :] = start[:, 128 * j : 128 * j + 128]
        return carry

    lax.fori_loop(0, 2, suffix, 0)

    def score(s, r):
        return dot(qbuf[s], kbuf[r], NT)

    def fold(s, r, sc):
        rows = pl.ds(s * 256, 256)
        before = m_ref[rows, :]
        after = jnp.maximum(before, jnp.max(sc, axis=1, keepdims=True) * C2)
        shrink = jnp.exp2(before - after)
        weight = jnp.exp2(sc * C2 - after[:, :1])
        l_ref[rows, :] = l_ref[rows, :] * shrink + jnp.sum(weight, axis=1, keepdims=True)
        m_ref[rows, :] = after
        more = dot(weight.astype(BF16), kbuf[r, :, 0:512], NN)
        for j in range(4):
            acc[j, rows, :] = acc[j, rows, :] * shrink + more[:, 128 * j : 128 * j + 128]

    def attend(todo):
        now = score(*todo[0])
        for n, (s, r) in enumerate(todo):
            later = score(*todo[n + 1]) if n + 1 < len(todo) else None
            fold(s, r, now)
            now = later

    kx, kc = {}, {}

    def from_z(r, xb):
        kz[r, xb].wait_recv()
        if r in (1, 2):
            ring(r + 1, xb, k_rows(r, xb), k_rows(r + 1, xb), kz_s, kz_r, kz)
        elif r in (7, 6):
            ring(r - 1, xb, k_rows(r, xb), k_rows(r - 1, xb), kz_s, kz_r, kz)
        elif (r, xb) in ((3, 0), (5, 1)):
            ring(4, xb, k_rows(r, xb), k_rows(4, xb), kz_s, kz_r, kz)
        if xb == 0:
            kx[r] = (
                send(kbuf.at[r, 0:64], kbuf.at[r, 128:192], kx_s.at[r, 0], kx_r.at[r, 0], same_x),
                send(kbuf.at[r, 0:64], kbuf.at[r, 192:256], kx_s.at[r, 1], kx_r.at[r, 1], other_x),
            )
        else:
            kc[r] = [
                send(kbuf.at[r, 0:128], kbuf.at[r, 256:384], kc_s.at[r, 0], kc_r.at[r, 0], sib)
            ]

    def from_x(r):
        for copy in kx[r]:
            copy.wait_recv()
        kc[r].append(
            send(kbuf.at[r, 128:256], kbuf.at[r, 384:512], kc_s.at[r, 1], kc_r.at[r, 1], sib)
        )

    def ready(r):
        for copy in kc[r]:
            copy.wait_recv()

    ox[0].wait_recv()
    for r in (1, 7):
        ring(r, 1, kbuf.at[0, 256:320], k_rows(r, 1), kz_s, kz_r, kz)
    from_z(1, 0)
    from_z(7, 0)
    ox[1].wait_recv()
    sib0 = send(kbuf.at[0, 256:384], kbuf.at[0, 384:512], kc_s.at[0, 0], kc_r.at[0, 0], sib)
    qp[0].wait_recv()
    q2 = [q_send(4, 1, 2, 0, yp)]
    qm[0].wait_recv()
    q2.append(q_send(5, 3, 2, 1, ym))
    sib0.wait_recv()
    attend([(0, 0)])
    from_z(1, 1)
    from_z(7, 1)
    from_z(2, 0)
    from_z(6, 0)
    from_x(1)
    from_x(7)
    qp[1].wait_recv()
    qm[1].wait_recv()
    attend([(1, 0), (3, 0)])
    from_z(2, 1)
    from_z(6, 1)
    ready(1)
    ready(7)
    local[3].wait()
    ws = []
    for d in (2, 1, 3):
        to = (y + d) % 4
        cols = pl.ds(pl.multiple_of(1024 * to, 1024), 1024)
        ws.append(
            send(w_in.at[:, cols], wbuf.at[80 * d : 80 * d + 80], w_s.at[d], w_r.at[d], dev(y_=to))
        )
    attend([(0, 1), (1, 1), (3, 1)])
    from_z(3, 0)
    from_z(5, 0)
    from_x(2)
    from_x(6)
    attend([(0, 7), (1, 7), (3, 7)])
    from_z(3, 1)
    from_z(5, 1)
    ready(2)
    ready(6)
    for copy in q2:
        copy.wait_recv()
    attend([(2, 0), (2, 1), (2, 7)])
    from_x(3)
    from_x(5)
    from_z(4, 0)
    from_z(4, 1)
    attend([(0, 2), (1, 2), (2, 2), (3, 2)])
    from_x(4)
    ready(3)
    ready(5)
    ready(4)

    def last(i, carry):
        r = 3 + i
        attend([(0, r), (1, r), (2, r), (3, r)])
        return carry

    lax.fori_loop(0, 4, last, 0)
    wbuf[0:80, :] = w_in[:, pl.ds(pl.multiple_of(1024 * y, 1024), 1024)]

    local[4].wait()

    heads_out = []
    for d in (2, 1, 3, 0):
        to = (y + d) % 4

        def up(i, carry):
            for n in range(4):
                h = to * 8 + i * 4 + n
                parts, logs = [], []
                for a in range(4):
                    rows = pl.ds(((y + 4 - a) % 4) * 256 + h, 8, stride=32)
                    tot = l_ref[rows, :]
                    inv = 1.0 / tot
                    parts.append(
                        jnp.concatenate([acc[j, rows, :] * inv for j in range(4)], axis=1)
                    )
                    logs.append(m_ref[rows, :] + jnp.log2(tot))
                attn = jnp.concatenate(parts, axis=0).astype(BF16)
                place = pl.ds(pl.multiple_of(i * 128 + n * 32, 32), 32)
                hv_send[d, place, :] = dot(attn, uv[h], NN).astype(BF16)
                lse_full[d, place, :] = jnp.concatenate(logs, axis=0)
            return carry

        lax.fori_loop(0, 2, up, 0)
        lse_send[d] = lse_full[d].T[0:8, :]
        if d:
            heads_out.append(
                (
                    send(hv_send.at[d], hv_recv.at[d], a_s.at[d, 0], a_r.at[d, 0], dev(y_=to)),
                    send(lse_send.at[d], lse_recv.at[d], a_s.at[d, 1], a_r.at[d, 1], dev(y_=to)),
                )
            )
    for pair in heads_out:
        for copy in pair:
            copy.wait_recv()
    logs = [lse_send[0]] + [lse_recv[d] for d in (1, 2, 3)]
    best = jnp.maximum(jnp.maximum(logs[0], logs[1]), jnp.maximum(logs[2], logs[3]))
    part = [jnp.exp2(x - best) for x in logs]
    norm = 1.0 / (part[0] + part[1] + part[2] + part[3])
    total = None
    for d in range(4):
        share = jnp.concatenate([part[d] * norm] * 16, axis=0).T
        term = share * (hv_send[0] if d == 0 else hv_recv[d]).astype(F32)
        total = term if d == 0 else total + term
    total = total.astype(BF16)
    for h in range(8):
        units[0, 0, :, 128 * h : 128 * h + 128] = total[32 * h : 32 * h + 32, :]

    hz = {}
    hx = send(units.at[0, 0], units.at[0, 1], h_s.at[0, 0], h_r.at[0, 0], across)
    for r in (1, 7):
        ring(r, 0, units.at[0, 0], units.at[r, 0], h_s, h_r, hz)

    def place_unit(r, xb):
        base = (xh if xb == 0 else 1 - xh) * 256 + ((z + 8 - r) % 8) * 8
        unit = units[r, xb].astype(F32)
        for a in range(4):
            hv_all[pl.ds(pl.multiple_of(base + 64 * a, 8), 8), :] = unit[8 * a : 8 * a + 8, :]

    place_unit(0, 0)
    hx.wait_recv()
    for r in (1, 7):
        ring(r, 1, units.at[0, 1], units.at[r, 1], h_s, h_r, hz)
    place_unit(0, 1)
    for r in (1, 7, 2, 6, 3, 5, 4):
        for xb in (0, 1):
            hz[r, xb].wait_recv()
            if r in (1, 2):
                ring(r + 1, xb, units.at[r, xb], units.at[r + 1, xb], h_s, h_r, hz)
            elif r in (7, 6):
                ring(r - 1, xb, units.at[r, xb], units.at[r - 1, xb], h_s, h_r, hz)
            elif (r, xb) in ((3, 0), (5, 1)):
                ring(4, xb, units.at[r, xb], units.at[4, xb], h_s, h_r, hz)
        for xb in (0, 1):
            place_unit(r, xb)

    for copy in ws:
        copy.wait_recv()
    back = []
    for dh in (3, 2, 1, 0):
        h = peer(0, dh)[0]
        rows = pl.ds(pl.multiple_of(128 * h, 128), 128)
        out_send[dh] = dot(wbuf[...], hv_all[rows, :].astype(BF16), NT).astype(BF16)
        for d in (2, 1, 3, 0):
            if d or dh:
                n = 4 * d + dh
                back.append(
                    send(
                        out_send.at[dh, 80 * d : 80 * d + 80], rs.at[n],
                        rs_s.at[n], rs_r.at[n], peer(d, dh),
                    )
                )
    result = out_send[0, 0:80, :].astype(F32)
    for copy in back:
        copy.wait_recv()
    for n in range(1, 16):
        result = result + rs[n].astype(F32)
    out_ref[...] = result.astype(BF16)
    for copy in sent:
        copy.wait_send()


def per_device(
    queries, prefix_latent, suffix_latent, suffix_len, prefix_blocks, caption_reach, w_uv, w_out
):
    dma = pltpu.SemaphoreType.DMA
    return pl.pallas_call(
        kernel,
        out_shape=jax.ShapeDtypeStruct((80, 128), BF16),
        in_specs=[pl.BlockSpec(memory_space=pl.ANY)] * 5
        + [pl.BlockSpec(memory_space=pltpu.SMEM)] * 3,
        out_specs=pl.BlockSpec(memory_space=pltpu.VMEM),
        scratch_shapes=[
            pltpu.VMEM((256, 576), BF16),
            pltpu.VMEM((576, 256), BF16),
            pltpu.VMEM((512, 576), BF16),
            pltpu.VMEM((32, 512, 128), BF16),
            pltpu.VMEM((80, 4096), BF16),
            pltpu.VMEM((4, 256, 640), BF16),
            pltpu.VMEM((8, 512, 640), BF16),
            pltpu.VMEM((4, 1024, 128), F32),
            pltpu.VMEM((1024, 128), F32),
            pltpu.VMEM((1024, 128), F32),
            pltpu.VMEM((320, 1024), BF16),
            pltpu.VMEM((4, 256, 128), BF16),
            pltpu.VMEM((4, 256, 128), F32),
            pltpu.VMEM((4, 8, 256), F32),
            pltpu.VMEM((4, 256, 128), BF16),
            pltpu.VMEM((4, 8, 256), F32),
            pltpu.VMEM((8, 2, 32, 1024), BF16),
            pltpu.VMEM((512, 1024), F32),
            pltpu.VMEM((4, 320, 128), BF16),
            pltpu.VMEM((16, 80, 128), BF16),
            dma((5,)),
            dma((8, 2)), dma((8, 2)),
            dma((8, 2)), dma((8, 2)),
            dma((8, 2)), dma((8, 2)),
            dma((6,)), dma((6,)),
            dma((4,)), dma((4,)),
            dma((4, 2)), dma((4, 2)),
            dma((8, 2)), dma((8, 2)),
            dma((16,)), dma((16,)),
        ],
        compiler_params=pltpu.CompilerParams(
            collective_id=0, has_side_effects=True, vmem_limit_bytes=56 * 2**20
        ),
    )(
        queries.reshape(256, 576),
        prefix_latent.T,
        suffix_latent.reshape(512, 576),
        w_uv,
        w_out.T,
        suffix_len,
        prefix_blocks,
        caption_reach,
    ).T


def solution(mesh):
    placed = (
        P("blk", "heads", None),
        P("blk", None),
        P("blk", None, None),
        P("blk"),
        P(),
        P("blk"),
        P("heads", None, None),
        P("heads", "blk"),
    )
    return jax.shard_map(
        per_device, mesh=mesh, in_specs=placed, out_specs=P("heads", "blk"), check_vma=False
    )
```

```python
import jax
import jax.numpy as jnp
from jax import lax
from jax.experimental import pallas as pl
from jax.experimental.pallas import tpu as pltpu
from jax.sharding import PartitionSpec as P

C2 = (192.0 ** -0.5) * 1.4426950408889634
NEG = -1.0e30
NT = (((1,), (1,)), ((), ()))
NN = (((1,), (0,)), ((), ()))
F32 = jnp.float32
BF16 = jnp.bfloat16
MESH = pl.DeviceIdType.MESH


def dot(a, b, dims):
    return lax.dot_general(a, b, dims, preferred_element_type=F32)


def kernel(
    q_hbm, k_hbm, s_hbm, uv_hbm, w_hbm, len_ref, blocks_ref, reach_ref, out_ref,
    q_in, k_in, s_in, uv, w_in,
    qbuf, kbuf, acc, m_ref, l_ref,
    wbuf, hv_send, lse_full, lse_send, hv_recv, lse_recv,
    units, hv_all, out_send, rs,
    in_sem, kz_s, kz_r, kx_s, kx_r, kc_s, kc_r, q_s, q_r, w_s, w_r,
    a_s, a_r, h_s, h_r, hx_s, hx_r, rs_s, rs_r,
):
    hd = lax.axis_index("heads")
    b = lax.axis_index("blk")
    p, c = hd // 2, hd % 2
    xh, y, z = b // 32, (b // 8) % 4, b % 8

    def dev(xh_=None, y_=None, z_=None, p_=None, c_=None):
        xx = xh if xh_ is None else xh_
        yy = y if y_ is None else y_
        zz = z if z_ is None else z_
        pp = p if p_ is None else p_
        cc = c if c_ is None else c_
        return (pp * 2 + cc, xx * 32 + yy * 8 + zz)

    zp, zm = dev(z_=(z + 1) % 8), dev(z_=(z + 7) % 8)
    same_x, other_x = dev(p_=1 - p), dev(xh_=1 - xh, p_=1 - p)
    sib, across = dev(c_=1 - c), dev(xh_=1 - xh)

    def peer(d, dh):
        return dev(
            y_=(y + 4 - d) % 4,
            p_=p if dh // 2 == 0 else 1 - p,
            c_=c if dh % 2 == 0 else 1 - c,
        )

    local = []
    for n, (src, dst) in enumerate(
        ((q_hbm, q_in), (k_hbm, k_in), (s_hbm, s_in), (w_hbm, w_in), (uv_hbm, uv))
    ):
        copy = pltpu.make_async_copy(src, dst, in_sem.at[n])
        copy.start()
        local.append(copy)

    partners = [zp, zm, other_x, across]
    partners += [peer(d, dh) for d in range(4) for dh in range(4) if d or dh]
    barrier = pltpu.get_barrier_semaphore()
    for who in partners:
        pl.semaphore_signal(barrier, inc=1, device_id=who, device_id_type=MESH)

    sent = []

    def send(src, dst, ssem, rsem, who):
        copy = pltpu.make_async_remote_copy(
            src_ref=src, dst_ref=dst, send_sem=ssem, recv_sem=rsem,
            device_id=who, device_id_type=MESH,
        )
        copy.start()
        sent.append(copy)
        return copy

    m_ref[...] = jnp.full_like(m_ref, NEG)
    l_ref[...] = jnp.zeros_like(l_ref)
    acc[...] = jnp.zeros_like(acc)
    lanes = lax.broadcasted_iota(jnp.int32, (1, 64), 1)
    local[1].wait()
    own = (lanes == blocks_ref[b]).astype(F32)
    turn = lax.broadcasted_iota(jnp.int32, (256, 256), 0) == lax.broadcasted_iota(
        jnp.int32, (256, 256), 1
    )
    kbuf[0, 0:256, 0:576] = dot(turn.astype(F32).astype(BF16), k_in[...], NT).astype(BF16)
    kbuf[0, 0:256, 576:640] = jnp.broadcast_to(own, (256, 64)).astype(BF16)
    local[0].wait()
    qbuf[0, :, 0:576] = q_in[...]
    for i in range(8):
        seen = jnp.where(lanes >= reach_ref[i], F32(NEG), F32(0.0))
        qbuf[0, 32 * i : 32 * i + 32, 576:640] = jnp.broadcast_to(seen, (32, 64)).astype(BF16)

    pl.semaphore_wait(barrier, len(partners))

    quarter = pl.ds(pl.multiple_of(128 * p + 64 * c, 64), 64)
    quarter_x = pl.ds(pl.multiple_of(128 * (1 - p) + 64 * c, 64), 64)
    yp, ym = dev(y_=(y + 1) % 4), dev(y_=(y + 3) % 4)
    kz = {}

    def ring(r, xb, src, dst, s_sem, r_sem, table):
        forward = r <= 3 or (r == 4 and xb == 0)
        table[r, xb] = send(src, dst, s_sem.at[r, xb], r_sem.at[r, xb], zp if forward else zm)

    def k_rows(r, xb):
        return kbuf.at[r, 64 * xb : 64 * xb + 64]

    def q_send(n, s_from, s_to, half, who):
        rows = slice(128 * half, 128 * half + 128)
        return send(qbuf.at[s_from, rows], qbuf.at[s_to, rows], q_s.at[n], q_r.at[n], who)

    ox = [
        send(kbuf.at[0, quarter_x], kbuf.at[0, 256:320], kx_s.at[0, 0], kx_r.at[0, 0], other_x)
    ]
    for r in (1, 7):
        ring(r, 0, kbuf.at[0, quarter], k_rows(r, 0), kz_s, kz_r, kz)
    qp = [q_send(0, 0, 1, 0, yp)]
    qm = [q_send(1, 0, 3, 1, ym)]
    ox.append(
        send(kbuf.at[0, quarter], kbuf.at[0, 320:384], kx_s.at[0, 1], kx_r.at[0, 1], other_x)
    )
    qp.append(q_send(2, 0, 1, 1, yp))
    qm.append(q_send(3, 0, 3, 0, ym))

    local[2].wait()

    def suffix(i, carry):
        for n in range(4):
            rows = pl.ds(pl.multiple_of(i * 128 + n * 32, 32), 32)
            toks = pl.ds(pl.multiple_of(i * 256 + n * 64, 64), 64)
            sc = dot(qbuf[0, rows, 0:576], s_in[toks, :], NT) * C2
            sc = jnp.where(lanes < len_ref[4 * i + n], sc, F32(NEG))
            top = jnp.max(sc, axis=1, keepdims=True)
            weight = jnp.exp2(sc - top)
            m_ref[rows, :] = jnp.broadcast_to(top, (32, 128))
            l_ref[rows, :] = jnp.broadcast_to(jnp.sum(weight, axis=1, keepdims=True), (32, 128))
            start = dot(weight.astype(BF16), s_in[toks, 0:512], NN)
            for j in range(4):
                acc[j, rows, :] = start[:, 128 * j : 128 * j + 128]
        return carry


    def score(s, r):
        return dot(qbuf[s], kbuf[r], NT)

    def fold(s, r, sc):
        rows = pl.ds(s * 256, 256)
        before = m_ref[rows, :]
        after = jnp.maximum(before, jnp.max(sc, axis=1, keepdims=True) * C2)
        shrink = jnp.exp2(before - after)
        weight = jnp.exp2(sc * C2 - after[:, :1])
        l_ref[rows, :] = l_ref[rows, :] * shrink + jnp.sum(weight, axis=1, keepdims=True)
        m_ref[rows, :] = after
        more = dot(weight.astype(BF16), kbuf[r, :, 0:512], NN)
        for j in range(4):
            acc[j, rows, :] = acc[j, rows, :] * shrink + more[:, 128 * j : 128 * j + 128]

    def attend(todo):
        now = score(*todo[0])
        for n, (s, r) in enumerate(todo):
            later = score(*todo[n + 1]) if n + 1 < len(todo) else None
            fold(s, r, now)
            now = later

    kx, kc = {}, {}

    def from_z(r, xb):
        kz[r, xb].wait_recv()
        if r in (1, 2):
            ring(r + 1, xb, k_rows(r, xb), k_rows(r + 1, xb), kz_s, kz_r, kz)
        elif r in (7, 6):
            ring(r - 1, xb, k_rows(r, xb), k_rows(r - 1, xb), kz_s, kz_r, kz)
        elif (r, xb) in ((3, 0), (5, 1)):
            ring(4, xb, k_rows(r, xb), k_rows(4, xb), kz_s, kz_r, kz)
        if xb == 0:
            kx[r] = (
                send(kbuf.at[r, 0:64], kbuf.at[r, 128:192], kx_s.at[r, 0], kx_r.at[r, 0], same_x),
                send(kbuf.at[r, 0:64], kbuf.at[r, 192:256], kx_s.at[r, 1], kx_r.at[r, 1], other_x),
            )
        else:
            kc[r] = [
                send(kbuf.at[r, 0:128], kbuf.at[r, 256:384], kc_s.at[r, 0], kc_r.at[r, 0], sib)
            ]

    def from_x(r):
        for copy in kx[r]:
            copy.wait_recv()
        kc[r].append(
            send(kbuf.at[r, 128:256], kbuf.at[r, 384:512], kc_s.at[r, 1], kc_r.at[r, 1], sib)
        )

    def ready(r):
        for copy in kc[r]:
            copy.wait_recv()

    ox[0].wait_recv()
    for r in (1, 7):
        ring(r, 1, kbuf.at[0, 256:320], k_rows(r, 1), kz_s, kz_r, kz)
    from_z(1, 0)
    from_z(7, 0)
    ox[1].wait_recv()
    sib0 = send(kbuf.at[0, 256:384], kbuf.at[0, 384:512], kc_s.at[0, 0], kc_r.at[0, 0], sib)
    qp[0].wait_recv()
    q2 = [q_send(4, 1, 2, 0, yp)]
    qm[0].wait_recv()
    q2.append(q_send(5, 3, 2, 1, ym))
    lax.fori_loop(0, 2, suffix, 0)
    sib0.wait_recv()
    attend([(0, 0)])
    for part in ((1, 1), (7, 1), (2, 0), (6, 0)):
        from_z(*part)
    from_x(1)
    from_x(7)
    qp[1].wait_recv()
    qm[1].wait_recv()
    attend([(1, 0), (3, 0)])
    ready(1)
    ready(7)
    attend([(0, 1), (1, 1), (3, 1)])
    for part in ((2, 1), (6, 1), (3, 0), (5, 0)):
        from_z(*part)
    from_x(2)
    from_x(6)
    attend([(0, 7), (1, 7), (3, 7)])
    for copy in q2:
        copy.wait_recv()
    local[3].wait()
    ws = []
    for d in (2, 1, 3):
        to = (y + d) % 4
        cols = pl.ds(pl.multiple_of(1024 * to, 1024), 1024)
        ws.append(
            send(w_in.at[:, cols], wbuf.at[80 * d : 80 * d + 80], w_s.at[d], w_r.at[d], dev(y_=to))
        )
    attend([(2, 0), (2, 1), (2, 7)])
    for part in ((3, 1), (5, 1), (4, 0)):
        from_z(*part)
    ready(2)
    ready(6)
    attend([(0, 2), (1, 2), (2, 2), (3, 2)])
    from_x(3)
    from_x(5)
    from_z(4, 1)
    from_x(4)
    ready(3)
    ready(5)

    def last(i, carry):
        r = jnp.where(i == 0, 6, 1 + 2 * i)
        attend([(0, r), (1, r), (2, r), (3, r)])
        return carry

    lax.fori_loop(0, 3, last, 0)
    ready(4)
    attend([(0, 4), (1, 4), (2, 4), (3, 4)])
    wbuf[0:80, :] = w_in[:, pl.ds(pl.multiple_of(1024 * y, 1024), 1024)]

    local[4].wait()

    heads_out = {}
    for half in (0, 1):
        heads_out[half] = []
        for d in (2, 1, 3, 0):
            to = (y + d) % 4
            for n in range(4):
                h = to * 8 + half * 4 + n
                parts, logs = [], []
                for a in range(4):
                    rows = pl.ds(((y + 4 - a) % 4) * 256 + h, 8, stride=32)
                    tot = l_ref[rows, :]
                    inv = 1.0 / tot
                    parts.append(
                        jnp.concatenate([acc[j, rows, :] * inv for j in range(4)], axis=1)
                    )
                    logs.append(m_ref[rows, :] + jnp.log2(tot))
                attn = jnp.concatenate(parts, axis=0).astype(BF16)
                hv_send[d, half, 32 * n : 32 * n + 32, :] = dot(attn, uv[h], NN).astype(BF16)
                lse_full[32 * n : 32 * n + 32, :] = jnp.concatenate(logs, axis=0)
            lse_send[d, half] = lse_full[...].T[0:8, :]
            if d:
                n = 2 * half
                who = dev(y_=to)
                heads_out[half] += [
                    send(hv_send.at[d, half], hv_recv.at[d, half], a_s.at[d, n], a_r.at[d, n], who),
                    send(
                        lse_send.at[d, half], lse_recv.at[d, half],
                        a_s.at[d, n + 1], a_r.at[d, n + 1], who,
                    ),
                ]

    hz, hx = {}, {}

    def z_ring(r, half, start):
        forward = r <= 3 or (r == 4 and half == 0)
        hz[r, half] = send(
            units.at[start, 0, half], units.at[r, 0, half],
            h_s.at[r, half], h_r.at[r, half], zp if forward else zm,
        )

    def cross(r, half):
        hx[r, half] = send(
            units.at[r, 0, half], units.at[r, 1, half], hx_s.at[r, half], hx_r.at[r, half], across
        )

    def place_unit(r, xb, half):
        base = (xh if xb == 0 else 1 - xh) * 256 + ((z + 8 - r) % 8) * 8
        unit = units[r, xb, half].astype(F32)
        for a in range(4):
            rows = pl.ds(pl.multiple_of(base + 64 * a, 8), 8)
            hv_all[rows, 512 * half : 512 * half + 512] = unit[8 * a : 8 * a + 8, :]

    for half in (0, 1):
        for copy in heads_out[half]:
            copy.wait_recv()
        logs = [lse_send[0, half]] + [lse_recv[d, half] for d in (1, 2, 3)]
        best = jnp.maximum(jnp.maximum(logs[0], logs[1]), jnp.maximum(logs[2], logs[3]))
        part = [jnp.exp2(x - best) for x in logs]
        norm = 1.0 / (part[0] + part[1] + part[2] + part[3])
        share = [jnp.concatenate([x * norm] * 16, axis=0).T for x in part]
        total = share[0] * hv_send[0, half].astype(F32)
        for d in (1, 2, 3):
            total = total + share[d] * hv_recv[d, half].astype(F32)
        total = total.astype(BF16)
        for h in range(4):
            units[0, 0, half, :, 128 * h : 128 * h + 128] = total[32 * h : 32 * h + 32, :]
        z_ring(1, half, 0)
        z_ring(7, half, 0)
        cross(0, half)
    place_unit(0, 0, 0)
    place_unit(0, 0, 1)
    before = [(0, 0), (0, 1)]
    for pair in ((1, 7), (2, 6), (3, 5), (4,)):
        for half in (0, 1):
            for r in pair:
                hz[r, half].wait_recv()
                if r in (1, 2):
                    z_ring(r + 1, half, r)
                elif r in (7, 6):
                    z_ring(r - 1, half, r)
                elif (r, half) in ((3, 0), (5, 1)):
                    z_ring(4, half, r)
                cross(r, half)
        for r in pair:
            place_unit(r, 0, 0)
            place_unit(r, 0, 1)
        if pair[0] > 1:
            for r, half in before:
                hx[r, half].wait_recv()
                place_unit(r, 1, half)
            before = []
        before += [(r, half) for r in pair for half in (0, 1)]
    for r, half in before:
        hx[r, half].wait_recv()
        place_unit(r, 1, half)

    for copy in ws:
        copy.wait_recv()
    back = []
    for dh in (3, 2, 1, 0):
        h = peer(0, dh)[0]
        rows = pl.ds(pl.multiple_of(128 * h, 128), 128)
        out_send[dh] = dot(wbuf[...], hv_all[rows, :].astype(BF16), NT).astype(BF16)
        for d in (2, 1, 3, 0):
            if d or dh:
                n = 4 * d + dh
                back.append(
                    send(
                        out_send.at[dh, 80 * d : 80 * d + 80], rs.at[n],
                        rs_s.at[n], rs_r.at[n], peer(d, dh),
                    )
                )
    result = out_send[0, 0:80, :].astype(F32)
    for copy in back:
        copy.wait_recv()
    for n in range(1, 16):
        result = result + rs[n].astype(F32)
    out_ref[...] = result.astype(BF16)
    for copy in sent:
        copy.wait_send()


def per_device(
    queries, prefix_latent, suffix_latent, suffix_len, prefix_blocks, caption_reach, w_uv, w_out
):
    dma = pltpu.SemaphoreType.DMA
    return pl.pallas_call(
        kernel,
        out_shape=jax.ShapeDtypeStruct((80, 128), BF16),
        in_specs=[pl.BlockSpec(memory_space=pl.ANY)] * 5
        + [pl.BlockSpec(memory_space=pltpu.SMEM)] * 3,
        out_specs=pl.BlockSpec(memory_space=pltpu.VMEM),
        scratch_shapes=[
            pltpu.VMEM((256, 576), BF16),
            pltpu.VMEM((576, 256), BF16),
            pltpu.VMEM((512, 576), BF16),
            pltpu.VMEM((32, 512, 128), BF16),
            pltpu.VMEM((80, 4096), BF16),
            pltpu.VMEM((4, 256, 640), BF16),
            pltpu.VMEM((8, 512, 640), BF16),
            pltpu.VMEM((4, 1024, 128), F32),
            pltpu.VMEM((1024, 128), F32),
            pltpu.VMEM((1024, 128), F32),
            pltpu.VMEM((320, 1024), BF16),
            pltpu.VMEM((4, 2, 128, 128), BF16),
            pltpu.VMEM((128, 128), F32),
            pltpu.VMEM((4, 2, 8, 128), F32),
            pltpu.VMEM((4, 2, 128, 128), BF16),
            pltpu.VMEM((4, 2, 8, 128), F32),
            pltpu.VMEM((8, 2, 2, 32, 512), BF16),
            pltpu.VMEM((512, 1024), F32),
            pltpu.VMEM((4, 320, 128), BF16),
            pltpu.VMEM((16, 80, 128), BF16),
            dma((5,)),
            dma((8, 2)), dma((8, 2)),
            dma((8, 2)), dma((8, 2)),
            dma((8, 2)), dma((8, 2)),
            dma((6,)), dma((6,)),
            dma((4,)), dma((4,)),
            dma((4, 4)), dma((4, 4)),
            dma((8, 2)), dma((8, 2)),
            dma((8, 2)), dma((8, 2)),
            dma((16,)), dma((16,)),
        ],
        compiler_params=pltpu.CompilerParams(
            collective_id=0, has_side_effects=True, vmem_limit_bytes=56 * 2**20
        ),
    )(
        queries.reshape(256, 576),
        prefix_latent.T,
        suffix_latent.reshape(512, 576),
        w_uv,
        w_out.T,
        suffix_len,
        prefix_blocks,
        caption_reach,
    ).T


def solution(mesh):
    placed = (
        P("blk", "heads", None),
        P("blk", None),
        P("blk", None, None),
        P("blk"),
        P(),
        P("blk"),
        P("heads", None, None),
        P("heads", "blk"),
    )
    return jax.shard_map(
        per_device, mesh=mesh, in_specs=placed, out_specs=P("heads", "blk"), check_vma=False
    )
```

```python
import jax
import jax.numpy as jnp
from jax import lax
from jax.experimental import pallas as pl
from jax.experimental.pallas import tpu as pltpu
from jax.sharding import PartitionSpec as P

C2 = (192.0 ** -0.5) * 1.4426950408889634
NEG = -1.0e30
NT = (((1,), (1,)), ((), ()))
NN = (((1,), (0,)), ((), ()))
F32 = jnp.float32
BF16 = jnp.bfloat16
MESH = pl.DeviceIdType.MESH


def dot(a, b, dims):
    return lax.dot_general(a, b, dims, preferred_element_type=F32)


def kernel(
    q_hbm, k_hbm, s_hbm, uv_hbm, w_hbm, len_ref, blocks_ref, reach_ref, out_ref,
    q_in, k_in, s_in, uv, w_in,
    qbuf, kbuf, acc, m_ref, l_ref,
    wbuf, hv_send, lse_full, lse_send, hv_recv, lse_recv,
    units, hv_all, out_send, rs,
    in_sem, kz_s, kz_r, kx_s, kx_r, kc_s, kc_r, q_s, q_r, w_s, w_r,
    a_s, a_r, h_s, h_r, hx_s, hx_r, rs_s, rs_r,
):
    hd = lax.axis_index("heads")
    b = lax.axis_index("blk")
    p, c = hd // 2, hd % 2
    xh, y, z = b // 32, (b // 8) % 4, b % 8

    def dev(xh_=None, y_=None, z_=None, p_=None, c_=None):
        xx = xh if xh_ is None else xh_
        yy = y if y_ is None else y_
        zz = z if z_ is None else z_
        pp = p if p_ is None else p_
        cc = c if c_ is None else c_
        return (pp * 2 + cc, xx * 32 + yy * 8 + zz)

    zp, zm = dev(z_=(z + 1) % 8), dev(z_=(z + 7) % 8)
    same_x, other_x = dev(p_=1 - p), dev(xh_=1 - xh, p_=1 - p)
    sib, across = dev(c_=1 - c), dev(xh_=1 - xh)

    def peer(d, dh):
        return dev(
            y_=(y + 4 - d) % 4,
            p_=p if dh // 2 == 0 else 1 - p,
            c_=c if dh % 2 == 0 else 1 - c,
        )

    local = []
    for n, (src, dst) in enumerate(
        ((q_hbm, q_in), (k_hbm, k_in), (s_hbm, s_in), (w_hbm, w_in), (uv_hbm, uv))
    ):
        copy = pltpu.make_async_copy(src, dst, in_sem.at[n])
        copy.start()
        local.append(copy)

    partners = [zp, zm, dev(z_=(z + 2) % 8), dev(z_=(z + 6) % 8), other_x, across]
    partners += [peer(d, dh) for d in range(4) for dh in range(4) if d or dh]
    barrier = pltpu.get_barrier_semaphore()
    for who in partners:
        pl.semaphore_signal(barrier, inc=1, device_id=who, device_id_type=MESH)

    sent = []

    def send(src, dst, ssem, rsem, who):
        copy = pltpu.make_async_remote_copy(
            src_ref=src, dst_ref=dst, send_sem=ssem, recv_sem=rsem,
            device_id=who, device_id_type=MESH,
        )
        copy.start()
        sent.append(copy)
        return copy

    m_ref[...] = jnp.full_like(m_ref, NEG)
    l_ref[...] = jnp.zeros_like(l_ref)
    acc[...] = jnp.zeros_like(acc)
    lanes = lax.broadcasted_iota(jnp.int32, (1, 64), 1)
    local[1].wait()
    own = (lanes == blocks_ref[b]).astype(F32)
    turn = lax.broadcasted_iota(jnp.int32, (256, 256), 0) == lax.broadcasted_iota(
        jnp.int32, (256, 256), 1
    )
    kbuf[0, 0:256, 0:576] = dot(turn.astype(F32).astype(BF16), k_in[...], NT).astype(BF16)
    kbuf[0, 0:256, 576:640] = jnp.broadcast_to(own, (256, 64)).astype(BF16)
    local[0].wait()
    qbuf[0, :, 0:576] = q_in[...]
    for i in range(8):
        seen = jnp.where(lanes >= reach_ref[i], F32(NEG), F32(0.0))
        qbuf[0, 32 * i : 32 * i + 32, 576:640] = jnp.broadcast_to(seen, (32, 64)).astype(BF16)

    pl.semaphore_wait(barrier, len(partners))

    def quarter(mine, piece):
        start = 128 * (p if mine else 1 - p) + 64 * c + 32 * piece
        return kbuf.at[0, pl.ds(pl.multiple_of(start, 32), 32)]

    yp, ym = dev(y_=(y + 1) % 4), dev(y_=(y + 3) % 4)
    kz = {}

    def k_rows(r, xb, piece):
        start = 32 * piece + (256 if r == 0 else 64 * xb)
        return kbuf.at[r, start : start + 32]

    def ring(r, xb, piece, src):
        forward = r <= 3 or (r == 4 and xb == 0)
        n = 2 * xb + piece
        kz[r, xb, piece] = send(
            src, k_rows(r, xb, piece), kz_s.at[r, n], kz_r.at[r, n], zp if forward else zm
        )

    def q_send(n, s_from, s_to, half, who):
        rows = slice(128 * half, 128 * half + 128)
        return send(qbuf.at[s_from, rows], qbuf.at[s_to, rows], q_s.at[n], q_r.at[n], who)

    ox = []
    for piece in (0, 1):
        ox.append(
            send(
                quarter(False, piece), k_rows(0, 1, piece),
                kx_s.at[0, piece], kx_r.at[0, piece], other_x,
            )
        )
        for r in (1, 7):
            ring(r, 0, piece, quarter(True, piece))
    qp = [q_send(0, 0, 1, 0, yp)]
    qm = [q_send(1, 0, 3, 1, ym)]
    whole = pl.ds(pl.multiple_of(128 * p + 64 * c, 64), 64)
    ox.append(
        send(kbuf.at[0, whole], kbuf.at[0, 320:384], kx_s.at[0, 2], kx_r.at[0, 2], other_x)
    )
    qp.append(q_send(2, 0, 1, 1, yp))
    qm.append(q_send(3, 0, 3, 0, ym))

    local[2].wait()

    def suffix(i, carry):
        for n in range(4):
            rows = pl.ds(pl.multiple_of(i * 128 + n * 32, 32), 32)
            toks = pl.ds(pl.multiple_of(i * 256 + n * 64, 64), 64)
            sc = dot(qbuf[0, rows, 0:576], s_in[toks, :], NT) * C2
            sc = jnp.where(lanes < len_ref[4 * i + n], sc, F32(NEG))
            top = jnp.max(sc, axis=1, keepdims=True)
            weight = jnp.exp2(sc - top)
            m_ref[rows, :] = jnp.broadcast_to(top, (32, 128))
            l_ref[rows, :] = jnp.broadcast_to(jnp.sum(weight, axis=1, keepdims=True), (32, 128))
            start = dot(weight.astype(BF16), s_in[toks, 0:512], NN)
            for j in range(4):
                acc[j, rows, :] = start[:, 128 * j : 128 * j + 128]
        return carry


    def score(s, r):
        return dot(qbuf[s], kbuf[r], NT)

    def fold(s, r, sc):
        rows = pl.ds(s * 256, 256)
        before = m_ref[rows, :]
        after = jnp.maximum(before, jnp.max(sc, axis=1, keepdims=True) * C2)
        shrink = jnp.exp2(before - after)
        weight = jnp.exp2(sc * C2 - after[:, :1])
        l_ref[rows, :] = l_ref[rows, :] * shrink + jnp.sum(weight, axis=1, keepdims=True)
        m_ref[rows, :] = after
        more = dot(weight.astype(BF16), kbuf[r, :, 0:512], NN)
        for j in range(4):
            acc[j, rows, :] = acc[j, rows, :] * shrink + more[:, 128 * j : 128 * j + 128]

    def attend(todo):
        now = score(*todo[0])
        for n, (s, r) in enumerate(todo):
            later = score(*todo[n + 1]) if n + 1 < len(todo) else None
            fold(s, r, now)
            now = later

    kx, kc = {}, {}

    def from_z(*parts):
        for piece in (0, 1):
            for r, xb in parts:
                kz[r, xb, piece].wait_recv()
                if r in (1, 2):
                    ring(r + 1, xb, piece, k_rows(r, xb, piece))
                elif r in (7, 6):
                    ring(r - 1, xb, piece, k_rows(r, xb, piece))
                elif (r, xb) in ((3, 0), (5, 1)):
                    ring(4, xb, piece, k_rows(r, xb, piece))
        for r, xb in parts:
            if xb == 0:
                half = kbuf.at[r, 0:64]
                kx[r] = (
                    send(half, kbuf.at[r, 128:192], kx_s.at[r, 0], kx_r.at[r, 0], same_x),
                    send(half, kbuf.at[r, 192:256], kx_s.at[r, 1], kx_r.at[r, 1], other_x),
                )
            else:
                kc[r] = [
                    send(kbuf.at[r, 0:128], kbuf.at[r, 256:384], kc_s.at[r, 0], kc_r.at[r, 0], sib)
                ]

    def from_x(r):
        for copy in kx[r]:
            copy.wait_recv()
        kc[r].append(
            send(kbuf.at[r, 128:256], kbuf.at[r, 384:512], kc_s.at[r, 1], kc_r.at[r, 1], sib)
        )

    def ready(r):
        for copy in kc[r]:
            copy.wait_recv()

    for piece in (0, 1):
        ox[piece].wait_recv()
        for r in (1, 7):
            ring(r, 1, piece, k_rows(0, 1, piece))
    from_z((1, 0), (7, 0))
    ox[2].wait_recv()
    sib0 = send(kbuf.at[0, 256:384], kbuf.at[0, 384:512], kc_s.at[0, 0], kc_r.at[0, 0], sib)
    qp[0].wait_recv()
    q2 = [q_send(4, 1, 2, 0, yp)]
    qm[0].wait_recv()
    q2.append(q_send(5, 3, 2, 1, ym))
    lax.fori_loop(0, 2, suffix, 0)
    from_z((1, 1), (7, 1))
    sib0.wait_recv()
    attend([(0, 0)])
    from_z((2, 0), (6, 0))
    from_x(1)
    from_x(7)
    qp[1].wait_recv()
    qm[1].wait_recv()
    attend([(1, 0), (3, 0)])
    from_z((2, 1), (6, 1))
    ready(1)
    ready(7)
    attend([(0, 1), (1, 1), (3, 1)])
    from_z((3, 0), (5, 0))
    from_x(2)
    from_x(6)
    attend([(0, 7), (1, 7), (3, 7)])
    for copy in q2:
        copy.wait_recv()
    from_z((3, 1), (5, 1))
    local[3].wait()
    ws = []
    for d in (2, 1, 3):
        to = (y + d) % 4
        cols = pl.ds(pl.multiple_of(1024 * to, 1024), 1024)
        ws.append(
            send(w_in.at[:, cols], wbuf.at[80 * d : 80 * d + 80], w_s.at[d], w_r.at[d], dev(y_=to))
        )
    attend([(2, 0), (2, 1), (2, 7)])
    from_z((4, 0))
    ready(2)
    ready(6)
    attend([(0, 2), (1, 2), (2, 2), (3, 2)])
    from_x(3)
    from_x(5)
    from_z((4, 1))
    attend([(0, 6), (1, 6), (2, 6), (3, 6)])
    ready(3)
    attend([(0, 3), (1, 3), (2, 3), (3, 3)])
    from_x(4)
    ready(5)
    attend([(0, 5), (1, 5), (2, 5), (3, 5)])
    ready(4)
    attend([(0, 4), (1, 4), (2, 4), (3, 4)])
    wbuf[0:80, :] = w_in[:, pl.ds(pl.multiple_of(1024 * y, 1024), 1024)]

    local[4].wait()

    heads_out = {}
    for half in (0, 1):
        heads_out[half] = []
        for d in (2, 1, 3, 0):
            to = (y + d) % 4
            for n in range(4):
                h = to * 8 + half * 4 + n
                parts, logs = [], []
                for a in range(4):
                    rows = pl.ds(((y + 4 - a) % 4) * 256 + h, 8, stride=32)
                    tot = l_ref[rows, :]
                    inv = 1.0 / tot
                    parts.append(
                        jnp.concatenate([acc[j, rows, :] * inv for j in range(4)], axis=1)
                    )
                    logs.append(m_ref[rows, :] + jnp.log2(tot))
                attn = jnp.concatenate(parts, axis=0).astype(BF16)
                hv_send[d, half, 32 * n : 32 * n + 32, :] = dot(attn, uv[h], NN).astype(BF16)
                lse_full[32 * n : 32 * n + 32, :] = jnp.concatenate(logs, axis=0)
            lse_send[d, half] = lse_full[...].T[0:8, :]
            if d:
                n = 2 * half
                who = dev(y_=to)
                heads_out[half] += [
                    send(hv_send.at[d, half], hv_recv.at[d, half], a_s.at[d, n], a_r.at[d, n], who),
                    send(
                        lse_send.at[d, half], lse_recv.at[d, half],
                        a_s.at[d, n + 1], a_r.at[d, n + 1], who,
                    ),
                ]

    hz, hx = {}, {}

    def along_z(r, half, start):
        steps = (r - start) % 8
        who = dev(z_=(z + steps) % 8)
        hz[r, half] = send(
            units.at[start, 0, half], units.at[r, 0, half],
            h_s.at[r, half], h_r.at[r, half], who,
        )

    def cross(r, half):
        hx[r, half] = send(
            units.at[r, 0, half], units.at[r, 1, half], hx_s.at[r, half], hx_r.at[r, half], across
        )

    def place_unit(r, xb, half):
        base = (xh if xb == 0 else 1 - xh) * 256 + ((z + 8 - r) % 8) * 8
        unit = units[r, xb, half].astype(F32)
        for a in range(4):
            rows = pl.ds(pl.multiple_of(base + 64 * a, 8), 8)
            hv_all[rows, 512 * half : 512 * half + 512] = unit[8 * a : 8 * a + 8, :]

    for half in (0, 1):
        for copy in heads_out[half]:
            copy.wait_recv()
        logs = [lse_send[0, half]] + [lse_recv[d, half] for d in (1, 2, 3)]
        best = jnp.maximum(jnp.maximum(logs[0], logs[1]), jnp.maximum(logs[2], logs[3]))
        part = [jnp.exp2(x - best) for x in logs]
        norm = 1.0 / (part[0] + part[1] + part[2] + part[3])
        share = [jnp.concatenate([x * norm] * 16, axis=0).T for x in part]
        total = share[0] * hv_send[0, half].astype(F32)
        for d in (1, 2, 3):
            total = total + share[d] * hv_recv[d, half].astype(F32)
        total = total.astype(BF16)
        for h in range(4):
            units[0, 0, half, :, 128 * h : 128 * h + 128] = total[32 * h : 32 * h + 32, :]
        for r in (2, 6, 1, 7):
            along_z(r, half, 0)
        cross(0, half)
    place_unit(0, 0, 0)
    place_unit(0, 0, 1)
    done = 0
    while done < len(sent) and sent[done] is not hz[2, 0]:
        sent[done].wait_send()
        done += 1
    for half in (0, 1):
        for r in (1, 7, 2, 6):
            hz[r, half].wait_recv()
            if r == 2:
                along_z(3, half, 2)
                if half == 0:
                    along_z(4, half, 2)
            elif r == 6:
                along_z(5, half, 6)
                if half == 1:
                    along_z(4, half, 6)
            cross(r, half)
    for r in (1, 7, 2, 6):
        for half in (0, 1):
            place_unit(r, 0, half)
    for r, half in ((0, 0), (0, 1), (1, 0), (7, 0)):
        hx[r, half].wait_recv()
        place_unit(r, 1, half)
    for r, half in ((3, 0), (5, 0), (4, 0), (3, 1), (5, 1), (4, 1)):
        hz[r, half].wait_recv()
        cross(r, half)
        place_unit(r, 0, half)
    for r, half in (
        (2, 0), (6, 0), (1, 1), (7, 1), (2, 1), (6, 1), (3, 0), (5, 0), (4, 0), (3, 1), (5, 1), (4, 1)
    ):
        hx[r, half].wait_recv()
        place_unit(r, 1, half)

    for copy in ws:
        copy.wait_recv()
    back = []
    for dh in (3, 2, 1, 0):
        h = peer(0, dh)[0]
        rows = pl.ds(pl.multiple_of(128 * h, 128), 128)
        out_send[dh] = dot(wbuf[...], hv_all[rows, :].astype(BF16), NT).astype(BF16)
        for d in (2, 1, 3, 0):
            if d or dh:
                n = 4 * d + dh
                back.append(
                    send(
                        out_send.at[dh, 80 * d : 80 * d + 80], rs.at[n],
                        rs_s.at[n], rs_r.at[n], peer(d, dh),
                    )
                )
    result = out_send[0, 0:80, :].astype(F32)
    for copy in sent[done : len(sent) - len(back)]:
        copy.wait_send()
    for copy in back:
        copy.wait_recv()
    for n in range(1, 16):
        result = result + rs[n].astype(F32)
    out_ref[...] = result.astype(BF16)
    for copy in back:
        copy.wait_send()


def per_device(
    queries, prefix_latent, suffix_latent, suffix_len, prefix_blocks, caption_reach, w_uv, w_out
):
    dma = pltpu.SemaphoreType.DMA
    return pl.pallas_call(
        kernel,
        out_shape=jax.ShapeDtypeStruct((80, 128), BF16),
        in_specs=[pl.BlockSpec(memory_space=pl.ANY)] * 5
        + [pl.BlockSpec(memory_space=pltpu.SMEM)] * 3,
        out_specs=pl.BlockSpec(memory_space=pltpu.VMEM),
        scratch_shapes=[
            pltpu.VMEM((256, 576), BF16),
            pltpu.VMEM((576, 256), BF16),
            pltpu.VMEM((512, 576), BF16),
            pltpu.VMEM((32, 512, 128), BF16),
            pltpu.VMEM((80, 4096), BF16),
            pltpu.VMEM((4, 256, 640), BF16),
            pltpu.VMEM((8, 512, 640), BF16),
            pltpu.VMEM((4, 1024, 128), F32),
            pltpu.VMEM((1024, 128), F32),
            pltpu.VMEM((1024, 128), F32),
            pltpu.VMEM((320, 1024), BF16),
            pltpu.VMEM((4, 2, 128, 128), BF16),
            pltpu.VMEM((128, 128), F32),
            pltpu.VMEM((4, 2, 8, 128), F32),
            pltpu.VMEM((4, 2, 128, 128), BF16),
            pltpu.VMEM((4, 2, 8, 128), F32),
            pltpu.VMEM((8, 2, 2, 32, 512), BF16),
            pltpu.VMEM((512, 1024), F32),
            pltpu.VMEM((4, 320, 128), BF16),
            pltpu.VMEM((16, 80, 128), BF16),
            dma((5,)),
            dma((8, 4)), dma((8, 4)),
            dma((8, 3)), dma((8, 3)),
            dma((8, 2)), dma((8, 2)),
            dma((6,)), dma((6,)),
            dma((4,)), dma((4,)),
            dma((4, 4)), dma((4, 4)),
            dma((8, 2)), dma((8, 2)),
            dma((8, 2)), dma((8, 2)),
            dma((16,)), dma((16,)),
        ],
        compiler_params=pltpu.CompilerParams(
            collective_id=0, has_side_effects=True, vmem_limit_bytes=56 * 2**20
        ),
    )(
        queries.reshape(256, 576),
        prefix_latent.T,
        suffix_latent.reshape(512, 576),
        w_uv,
        w_out.T,
        suffix_len,
        prefix_blocks,
        caption_reach,
    ).T


def solution(mesh):
    placed = (
        P("blk", "heads", None),
        P("blk", None),
        P("blk", None, None),
        P("blk"),
        P(),
        P("blk"),
        P("heads", None, None),
        P("heads", "blk"),
    )
    return jax.shard_map(
        per_device, mesh=mesh, in_specs=placed, out_specs=P("heads", "blk"), check_vma=False
    )
```

```python
import jax
import jax.numpy as jnp
from jax import lax
from jax.experimental import pallas as pl
from jax.experimental.pallas import tpu as pltpu
from jax.sharding import PartitionSpec as P

C2 = (192.0 ** -0.5) * 1.4426950408889634
NEG = -1.0e30
NT = (((1,), (1,)), ((), ()))
NN = (((1,), (0,)), ((), ()))
F32 = jnp.float32
BF16 = jnp.bfloat16
MESH = pl.DeviceIdType.MESH


def dot(a, b, dims):
    return lax.dot_general(a, b, dims, preferred_element_type=F32)


def kernel(
    q_hbm, k_hbm, s_hbm, uv_hbm, w_hbm, len_ref, blocks_ref, reach_ref, out_ref,
    q_in, k_in, s_in, uv, w_in,
    qbuf, kbuf, acc, m_ref, l_ref,
    wbuf, hv_send, lse_full, lse_send, hv_recv, lse_recv,
    units, hv_all, out_send, rs,
    in_sem, kz_s, kz_r, kx_s, kx_r, kc_s, kc_r, q_s, q_r, w_s, w_r,
    a_s, a_r, h_s, h_r, hx_s, hx_r, rs_s, rs_r,
):
    hd = lax.axis_index("heads")
    b = lax.axis_index("blk")
    p, c = hd // 2, hd % 2
    xh, y, z = b // 32, (b // 8) % 4, b % 8

    def dev(xh_=None, y_=None, z_=None, p_=None, c_=None):
        xx = xh if xh_ is None else xh_
        yy = y if y_ is None else y_
        zz = z if z_ is None else z_
        pp = p if p_ is None else p_
        cc = c if c_ is None else c_
        return (pp * 2 + cc, xx * 32 + yy * 8 + zz)

    zp, zm = dev(z_=(z + 1) % 8), dev(z_=(z + 7) % 8)
    same_x, other_x = dev(p_=1 - p), dev(xh_=1 - xh, p_=1 - p)
    sib, across = dev(c_=1 - c), dev(xh_=1 - xh)

    def peer(d, dh):
        return dev(
            y_=(y + 4 - d) % 4,
            p_=p if dh // 2 == 0 else 1 - p,
            c_=c if dh % 2 == 0 else 1 - c,
        )

    local = []
    for n, (src, dst) in enumerate(
        ((q_hbm, q_in), (k_hbm, k_in), (s_hbm, s_in), (w_hbm, w_in), (uv_hbm, uv))
    ):
        copy = pltpu.make_async_copy(src, dst, in_sem.at[n])
        copy.start()
        local.append(copy)

    partners = [zp, zm, dev(z_=(z + 2) % 8), dev(z_=(z + 6) % 8), other_x, across]
    partners += [peer(d, dh) for d in range(4) for dh in range(4) if d or dh]
    barrier = pltpu.get_barrier_semaphore()
    for who in partners:
        pl.semaphore_signal(barrier, inc=1, device_id=who, device_id_type=MESH)

    sent = []

    def send(src, dst, ssem, rsem, who):
        copy = pltpu.make_async_remote_copy(
            src_ref=src, dst_ref=dst, send_sem=ssem, recv_sem=rsem,
            device_id=who, device_id_type=MESH,
        )
        copy.start()
        sent.append(copy)
        return copy

    m_ref[...] = jnp.full_like(m_ref, NEG)
    l_ref[...] = jnp.zeros_like(l_ref)
    acc[...] = jnp.zeros_like(acc)
    lanes = lax.broadcasted_iota(jnp.int32, (1, 64), 1)
    local[1].wait()
    own = (lanes == blocks_ref[b]).astype(F32)
    turn = lax.broadcasted_iota(jnp.int32, (256, 256), 0) == lax.broadcasted_iota(
        jnp.int32, (256, 256), 1
    )
    kbuf[0, 0:256, 0:576] = dot(turn.astype(F32).astype(BF16), k_in[...], NT).astype(BF16)
    kbuf[0, 0:256, 576:640] = jnp.broadcast_to(own, (256, 64)).astype(BF16)
    local[0].wait()
    qbuf[0, :, 0:576] = q_in[...]
    for i in range(8):
        seen = jnp.where(lanes >= reach_ref[i], F32(NEG), F32(0.0))
        qbuf[0, 32 * i : 32 * i + 32, 576:640] = jnp.broadcast_to(seen, (32, 64)).astype(BF16)

    pl.semaphore_wait(barrier, len(partners))

    def quarter(mine, piece):
        start = 128 * (p if mine else 1 - p) + 64 * c + 32 * piece
        return kbuf.at[0, pl.ds(pl.multiple_of(start, 32), 32)]

    yp, ym = dev(y_=(y + 1) % 4), dev(y_=(y + 3) % 4)
    kz = {}

    def k_rows(r, xb, piece):
        start = 32 * piece + (256 if r == 0 else 64 * xb)
        return kbuf.at[r, start : start + 32]

    def ring(r, xb, piece, src):
        forward = r <= 3 or (r == 4 and xb == 0)
        n = 2 * xb + piece
        kz[r, xb, piece] = send(
            src, k_rows(r, xb, piece), kz_s.at[r, n], kz_r.at[r, n], zp if forward else zm
        )

    def q_send(n, s_from, s_to, half, who):
        rows = slice(128 * half, 128 * half + 128)
        return send(qbuf.at[s_from, rows], qbuf.at[s_to, rows], q_s.at[n], q_r.at[n], who)

    ox = []
    for piece in (0, 1):
        ox.append(
            send(
                quarter(False, piece), k_rows(0, 1, piece),
                kx_s.at[0, piece], kx_r.at[0, piece], other_x,
            )
        )
        for r in (1, 7):
            ring(r, 0, piece, quarter(True, piece))
    qp = [q_send(0, 0, 1, 0, yp)]
    qm = [q_send(1, 0, 3, 1, ym)]
    whole = pl.ds(pl.multiple_of(128 * p + 64 * c, 64), 64)
    ox.append(
        send(kbuf.at[0, whole], kbuf.at[0, 320:384], kx_s.at[0, 2], kx_r.at[0, 2], other_x)
    )
    qp.append(q_send(2, 0, 1, 1, yp))
    qm.append(q_send(3, 0, 3, 0, ym))

    local[2].wait()

    def suffix(i, carry):
        for n in range(4):
            rows = pl.ds(pl.multiple_of(i * 128 + n * 32, 32), 32)
            toks = pl.ds(pl.multiple_of(i * 256 + n * 64, 64), 64)
            sc = dot(qbuf[0, rows, 0:576], s_in[toks, :], NT) * C2
            sc = jnp.where(lanes < len_ref[4 * i + n], sc, F32(NEG))
            top = jnp.max(sc, axis=1, keepdims=True)
            weight = jnp.exp2(sc - top)
            m_ref[rows, :] = jnp.broadcast_to(top, (32, 128))
            l_ref[rows, :] = jnp.broadcast_to(jnp.sum(weight, axis=1, keepdims=True), (32, 128))
            start = dot(weight.astype(BF16), s_in[toks, 0:512], NN)
            for j in range(4):
                acc[j, rows, :] = start[:, 128 * j : 128 * j + 128]
        return carry


    def score(s, r):
        return dot(qbuf[s], kbuf[r], NT)

    def fold(s, r, sc):
        rows = pl.ds(s * 256, 256)
        before = m_ref[rows, :]
        after = jnp.maximum(before, jnp.max(sc, axis=1, keepdims=True) * C2)
        shrink = jnp.exp2(before - after)
        weight = jnp.exp2(sc * C2 - after[:, :1])
        l_ref[rows, :] = l_ref[rows, :] * shrink + jnp.sum(weight, axis=1, keepdims=True)
        m_ref[rows, :] = after
        more = dot(weight.astype(BF16), kbuf[r, :, 0:512], NN)
        for j in range(4):
            acc[j, rows, :] = acc[j, rows, :] * shrink + more[:, 128 * j : 128 * j + 128]

    def attend(todo):
        now = score(*todo[0])
        for n, (s, r) in enumerate(todo):
            later = score(*todo[n + 1]) if n + 1 < len(todo) else None
            fold(s, r, now)
            now = later

    kx, kc = {}, {}

    def from_z(*parts):
        for piece in (0, 1):
            for r, xb in parts:
                kz[r, xb, piece].wait_recv()
                if r in (1, 2):
                    ring(r + 1, xb, piece, k_rows(r, xb, piece))
                elif r in (7, 6):
                    ring(r - 1, xb, piece, k_rows(r, xb, piece))
                elif (r, xb) in ((3, 0), (5, 1)):
                    ring(4, xb, piece, k_rows(r, xb, piece))
        for r, xb in parts:
            if xb == 0:
                half = kbuf.at[r, 0:64]
                kx[r] = (
                    send(half, kbuf.at[r, 128:192], kx_s.at[r, 0], kx_r.at[r, 0], same_x),
                    send(half, kbuf.at[r, 192:256], kx_s.at[r, 1], kx_r.at[r, 1], other_x),
                )
            else:
                kc[r] = [
                    send(kbuf.at[r, 0:128], kbuf.at[r, 256:384], kc_s.at[r, 0], kc_r.at[r, 0], sib)
                ]

    def from_x(r):
        for copy in kx[r]:
            copy.wait_recv()
        kc[r].append(
            send(kbuf.at[r, 128:256], kbuf.at[r, 384:512], kc_s.at[r, 1], kc_r.at[r, 1], sib)
        )

    def ready(r):
        for copy in kc[r]:
            copy.wait_recv()

    for piece in (0, 1):
        ox[piece].wait_recv()
        for r in (1, 7):
            ring(r, 1, piece, k_rows(0, 1, piece))
    from_z((1, 0), (7, 0))
    ox[2].wait_recv()
    sib0 = send(kbuf.at[0, 256:384], kbuf.at[0, 384:512], kc_s.at[0, 0], kc_r.at[0, 0], sib)
    qp[0].wait_recv()
    q2 = [q_send(4, 1, 2, 0, yp)]
    qm[0].wait_recv()
    q2.append(q_send(5, 3, 2, 1, ym))
    lax.fori_loop(0, 2, suffix, 0)
    from_z((1, 1), (7, 1))
    sib0.wait_recv()
    attend([(0, 0)])
    from_z((2, 0), (6, 0))
    from_x(1)
    from_x(7)
    qp[1].wait_recv()
    qm[1].wait_recv()
    attend([(1, 0), (3, 0)])
    from_z((2, 1), (6, 1))
    ready(1)
    ready(7)
    attend([(0, 1), (1, 1), (3, 1)])
    from_z((3, 0), (5, 0))
    from_x(2)
    from_x(6)
    attend([(0, 7), (1, 7), (3, 7)])
    for copy in q2:
        copy.wait_recv()
    from_z((3, 1), (5, 1))
    local[3].wait()
    ws = []
    for d in (2, 1, 3):
        to = (y + d) % 4
        cols = pl.ds(pl.multiple_of(1024 * to, 1024), 1024)
        ws.append(
            send(w_in.at[:, cols], wbuf.at[80 * d : 80 * d + 80], w_s.at[d], w_r.at[d], dev(y_=to))
        )
    attend([(2, 0), (2, 1), (2, 7)])
    from_z((4, 0))
    ready(2)
    ready(6)
    attend([(0, 2), (1, 2), (2, 2), (3, 2)])
    from_x(3)
    from_x(5)
    from_z((4, 1))
    attend([(0, 6), (1, 6), (2, 6), (3, 6)])
    ready(3)
    attend([(0, 3), (1, 3), (2, 3), (3, 3)])
    from_x(4)
    ready(5)
    attend([(0, 5), (1, 5), (2, 5), (3, 5)])
    ready(4)
    attend([(0, 4), (1, 4), (2, 4), (3, 4)])
    wbuf[0:80, :] = w_in[:, pl.ds(pl.multiple_of(1024 * y, 1024), 1024)]

    local[4].wait()

    heads_out = {}
    for half in (0, 1):
        heads_out[half] = []
        for d in (2, 1, 3, 0):
            to = (y + d) % 4
            for n in range(4):
                h = to * 8 + half * 4 + n
                parts, logs = [], []
                for a in range(4):
                    rows = pl.ds(((y + 4 - a) % 4) * 256 + h, 8, stride=32)
                    tot = l_ref[rows, :]
                    inv = 1.0 / tot
                    parts.append(
                        jnp.concatenate([acc[j, rows, :] * inv for j in range(4)], axis=1)
                    )
                    logs.append(m_ref[rows, :] + jnp.log2(tot))
                attn = jnp.concatenate(parts, axis=0).astype(BF16)
                hv_send[d, half, 32 * n : 32 * n + 32, :] = dot(attn, uv[h], NN).astype(BF16)
                lse_full[32 * n : 32 * n + 32, :] = jnp.concatenate(logs, axis=0)
            lse_send[d, half] = lse_full[...].T[0:8, :]
            if d:
                n = 2 * half
                who = dev(y_=to)
                heads_out[half] += [
                    send(hv_send.at[d, half], hv_recv.at[d, half], a_s.at[d, n], a_r.at[d, n], who),
                    send(
                        lse_send.at[d, half], lse_recv.at[d, half],
                        a_s.at[d, n + 1], a_r.at[d, n + 1], who,
                    ),
                ]

    hz, hx = {}, {}

    def along_z(r, half, start):
        steps = (r - start) % 8
        who = dev(z_=(z + steps) % 8)
        hz[r, half] = send(
            units.at[start, 0, half], units.at[r, 0, half],
            h_s.at[r, half], h_r.at[r, half], who,
        )

    def crossed_along_z(r, half, start):
        hx[r, half] = send(
            units.at[start, 1, half], units.at[r, 1, half],
            hx_s.at[r, half], hx_r.at[r, half], zp if r in (1, 3) else zm,
        )

    def cross(r, half):
        hx[r, half] = send(
            units.at[r, 0, half], units.at[r, 1, half], hx_s.at[r, half], hx_r.at[r, half], across
        )

    def place_unit(r, xb, half):
        base = (xh if xb == 0 else 1 - xh) * 256 + ((z + 8 - r) % 8) * 8
        unit = units[r, xb, half].astype(F32)
        for a in range(4):
            rows = pl.ds(pl.multiple_of(base + 64 * a, 8), 8)
            hv_all[rows, 512 * half : 512 * half + 512] = unit[8 * a : 8 * a + 8, :]

    for half in (0, 1):
        for copy in heads_out[half]:
            copy.wait_recv()
        logs = [lse_send[0, half]] + [lse_recv[d, half] for d in (1, 2, 3)]
        best = jnp.maximum(jnp.maximum(logs[0], logs[1]), jnp.maximum(logs[2], logs[3]))
        part = [jnp.exp2(x - best) for x in logs]
        norm = 1.0 / (part[0] + part[1] + part[2] + part[3])
        share = [jnp.concatenate([x * norm] * 16, axis=0).T for x in part]
        total = share[0] * hv_send[0, half].astype(F32)
        for d in (1, 2, 3):
            total = total + share[d] * hv_recv[d, half].astype(F32)
        total = total.astype(BF16)
        for h in range(4):
            units[0, 0, half, :, 128 * h : 128 * h + 128] = total[32 * h : 32 * h + 32, :]
        for r in (2, 6, 1, 7):
            along_z(r, half, 0)
        cross(0, half)
    place_unit(0, 0, 0)
    place_unit(0, 0, 1)
    done = 0
    while done < len(sent) and sent[done] is not hz[2, 0]:
        sent[done].wait_send()
        done += 1
    for half in (0, 1):
        for r in (1, 7, 2, 6):
            hz[r, half].wait_recv()
            if r == 2:
                along_z(3, half, 2)
                if half == 0:
                    along_z(4, half, 2)
            elif r == 6:
                along_z(5, half, 6)
                if half == 1:
                    along_z(4, half, 6)
            if r in (2, 6):
                cross(r, half)
    for half in (0, 1):
        hx[0, half].wait_recv()
        for r in (1, 7):
            crossed_along_z(r, half, 0)
    for r in (1, 7, 2, 6):
        for half in (0, 1):
            place_unit(r, 0, half)
    for half in (0, 1):
        place_unit(0, 1, half)
    for half in (0, 1):
        hx[2, half].wait_recv()
        crossed_along_z(3, half, 2)
        hx[6, half].wait_recv()
        crossed_along_z(5, half, 6)
        hz[4, half].wait_recv()
        cross(4, half)
        for r in (2, 6):
            place_unit(r, 1, half)
    for r, half in ((4, 0), (4, 1)):
        place_unit(r, 0, half)
    for r, half in ((3, 0), (5, 0), (3, 1), (5, 1)):
        hz[r, half].wait_recv()
        place_unit(r, 0, half)
    for r, half in (
        (1, 0), (7, 0), (1, 1), (7, 1), (3, 0), (5, 0), (4, 0), (3, 1), (5, 1), (4, 1)
    ):
        hx[r, half].wait_recv()
        place_unit(r, 1, half)

    for copy in ws:
        copy.wait_recv()
    back = []
    for dh in (3, 2, 1, 0):
        h = peer(0, dh)[0]
        rows = pl.ds(pl.multiple_of(128 * h, 128), 128)
        out_send[dh] = dot(wbuf[...], hv_all[rows, :].astype(BF16), NT).astype(BF16)
        for d in (2, 1, 3, 0):
            if d or dh:
                n = 4 * d + dh
                back.append(
                    send(
                        out_send.at[dh, 80 * d : 80 * d + 80], rs.at[n],
                        rs_s.at[n], rs_r.at[n], peer(d, dh),
                    )
                )
    result = out_send[0, 0:80, :].astype(F32)
    for copy in sent[done : len(sent) - len(back)]:
        copy.wait_send()
    for copy in back:
        copy.wait_recv()
    for n in range(1, 16):
        result = result + rs[n].astype(F32)
    out_ref[...] = result.astype(BF16)
    for copy in back:
        copy.wait_send()


def per_device(
    queries, prefix_latent, suffix_latent, suffix_len, prefix_blocks, caption_reach, w_uv, w_out
):
    dma = pltpu.SemaphoreType.DMA
    return pl.pallas_call(
        kernel,
        out_shape=jax.ShapeDtypeStruct((80, 128), BF16),
        in_specs=[pl.BlockSpec(memory_space=pl.ANY)] * 5
        + [pl.BlockSpec(memory_space=pltpu.SMEM)] * 3,
        out_specs=pl.BlockSpec(memory_space=pltpu.VMEM),
        scratch_shapes=[
            pltpu.VMEM((256, 576), BF16),
            pltpu.VMEM((576, 256), BF16),
            pltpu.VMEM((512, 576), BF16),
            pltpu.VMEM((32, 512, 128), BF16),
            pltpu.VMEM((80, 4096), BF16),
            pltpu.VMEM((4, 256, 640), BF16),
            pltpu.VMEM((8, 512, 640), BF16),
            pltpu.VMEM((4, 1024, 128), F32),
            pltpu.VMEM((1024, 128), F32),
            pltpu.VMEM((1024, 128), F32),
            pltpu.VMEM((320, 1024), BF16),
            pltpu.VMEM((4, 2, 128, 128), BF16),
            pltpu.VMEM((128, 128), F32),
            pltpu.VMEM((4, 2, 8, 128), F32),
            pltpu.VMEM((4, 2, 128, 128), BF16),
            pltpu.VMEM((4, 2, 8, 128), F32),
            pltpu.VMEM((8, 2, 2, 32, 512), BF16),
            pltpu.VMEM((512, 1024), F32),
            pltpu.VMEM((4, 320, 128), BF16),
            pltpu.VMEM((16, 80, 128), BF16),
            dma((5,)),
            dma((8, 4)), dma((8, 4)),
            dma((8, 3)), dma((8, 3)),
            dma((8, 2)), dma((8, 2)),
            dma((6,)), dma((6,)),
            dma((4,)), dma((4,)),
            dma((4, 4)), dma((4, 4)),
            dma((8, 2)), dma((8, 2)),
            dma((8, 2)), dma((8, 2)),
            dma((16,)), dma((16,)),
        ],
        compiler_params=pltpu.CompilerParams(
            collective_id=0, has_side_effects=True, vmem_limit_bytes=56 * 2**20
        ),
    )(
        queries.reshape(256, 576),
        prefix_latent.T,
        suffix_latent.reshape(512, 576),
        w_uv,
        w_out.T,
        suffix_len,
        prefix_blocks,
        caption_reach,
    ).T


def solution(mesh):
    placed = (
        P("blk", "heads", None),
        P("blk", None),
        P("blk", None, None),
        P("blk"),
        P(),
        P("blk"),
        P("heads", None, None),
        P("heads", "blk"),
    )
    return jax.shard_map(
        per_device, mesh=mesh, in_specs=placed, out_specs=P("heads", "blk"), check_vma=False
    )
```

```python
import jax
import jax.numpy as jnp
from jax import lax
from jax.experimental import pallas as pl
from jax.experimental.pallas import tpu as pltpu
from jax.sharding import PartitionSpec as P

C2 = (192.0 ** -0.5) * 1.4426950408889634
NEG = -1.0e30
NT = (((1,), (1,)), ((), ()))
NN = (((1,), (0,)), ((), ()))
F32 = jnp.float32
BF16 = jnp.bfloat16
MESH = pl.DeviceIdType.MESH


def dot(a, b, dims):
    return lax.dot_general(a, b, dims, preferred_element_type=F32)


def kernel(
    q_hbm, k_hbm, s_hbm, uv_hbm, w_hbm, len_ref, blocks_ref, reach_ref, out_ref,
    q_in, k_in, s_in, uv, w_in,
    qbuf, kbuf, acc, m_ref, l_ref,
    wbuf, hv_send, lse_full, lse_send, hv_recv, lse_recv,
    units, hv_all, out_send, rs,
    in_sem, kz_s, kz_r, kx_s, kx_r, kc_s, kc_r, q_s, q_r, w_s, w_r,
    a_s, a_r, h_s, h_r, hx_s, hx_r, rs_s, rs_r,
):
    hd = lax.axis_index("heads")
    b = lax.axis_index("blk")
    p, c = hd // 2, hd % 2
    xh, y, z = b // 32, (b // 8) % 4, b % 8

    def dev(xh_=None, y_=None, z_=None, p_=None, c_=None):
        xx = xh if xh_ is None else xh_
        yy = y if y_ is None else y_
        zz = z if z_ is None else z_
        pp = p if p_ is None else p_
        cc = c if c_ is None else c_
        return (pp * 2 + cc, xx * 32 + yy * 8 + zz)

    zp, zm = dev(z_=(z + 1) % 8), dev(z_=(z + 7) % 8)
    same_x, other_x = dev(p_=1 - p), dev(xh_=1 - xh, p_=1 - p)
    sib, across = dev(c_=1 - c), dev(xh_=1 - xh)

    def peer(d, dh):
        return dev(
            y_=(y + 4 - d) % 4,
            p_=p if dh // 2 == 0 else 1 - p,
            c_=c if dh % 2 == 0 else 1 - c,
        )

    local = []
    for n, (src, dst) in enumerate(
        ((q_hbm, q_in), (k_hbm, k_in), (s_hbm, s_in), (w_hbm, w_in), (uv_hbm, uv))
    ):
        copy = pltpu.make_async_copy(src, dst, in_sem.at[n])
        copy.start()
        local.append(copy)

    partners = [zp, zm, dev(z_=(z + 2) % 8), dev(z_=(z + 6) % 8), other_x, across]
    partners += [peer(d, dh) for d in range(4) for dh in range(4) if d or dh]
    barrier = pltpu.get_barrier_semaphore()
    for who in partners:
        pl.semaphore_signal(barrier, inc=1, device_id=who, device_id_type=MESH)

    sent = []

    def send(src, dst, ssem, rsem, who):
        copy = pltpu.make_async_remote_copy(
            src_ref=src, dst_ref=dst, send_sem=ssem, recv_sem=rsem,
            device_id=who, device_id_type=MESH,
        )
        copy.start()
        sent.append(copy)
        return copy

    lanes = lax.broadcasted_iota(jnp.int32, (1, 64), 1)
    local[1].wait()
    own = (lanes == blocks_ref[b]).astype(F32)
    turn = lax.broadcasted_iota(jnp.int32, (256, 256), 0) == lax.broadcasted_iota(
        jnp.int32, (256, 256), 1
    )
    kbuf[0, 0:256, 0:576] = dot(turn.astype(F32).astype(BF16), k_in[...], NT).astype(BF16)
    kbuf[0, 0:256, 576:640] = jnp.broadcast_to(own, (256, 64)).astype(BF16)
    local[0].wait()
    qbuf[0, :, 0:576] = q_in[...]
    for i in range(8):
        seen = jnp.where(lanes >= reach_ref[i], F32(NEG), F32(0.0))
        qbuf[0, 32 * i : 32 * i + 32, 576:640] = jnp.broadcast_to(seen, (32, 64)).astype(BF16)

    pl.semaphore_wait(barrier, len(partners))

    def quarter(mine, piece):
        start = 128 * (p if mine else 1 - p) + 64 * c + 32 * piece
        return kbuf.at[0, pl.ds(pl.multiple_of(start, 32), 32)]

    yp, ym = dev(y_=(y + 1) % 4), dev(y_=(y + 3) % 4)
    kz = {}

    def k_rows(r, xb, piece):
        start = 32 * piece + (256 if r == 0 else 64 * xb)
        return kbuf.at[r, start : start + 32]

    def ring(r, xb, piece, src):
        forward = r <= 3 or (r == 4 and xb == 0)
        n = 2 * xb + piece
        kz[r, xb, piece] = send(
            src, k_rows(r, xb, piece), kz_s.at[r, n], kz_r.at[r, n], zp if forward else zm
        )

    def q_send(n, s_from, s_to, half, who):
        rows = slice(128 * half, 128 * half + 128)
        return send(qbuf.at[s_from, rows], qbuf.at[s_to, rows], q_s.at[n], q_r.at[n], who)

    ox = []
    for piece in (0, 1):
        ox.append(
            send(
                quarter(False, piece), k_rows(0, 1, piece),
                kx_s.at[0, piece], kx_r.at[0, piece], other_x,
            )
        )
        for r in (1, 7):
            ring(r, 0, piece, quarter(True, piece))
    qp = [q_send(0, 0, 1, 0, yp)]
    qm = [q_send(1, 0, 3, 1, ym)]
    whole = pl.ds(pl.multiple_of(128 * p + 64 * c, 64), 64)
    ox.append(
        send(kbuf.at[0, whole], kbuf.at[0, 320:384], kx_s.at[0, 2], kx_r.at[0, 2], other_x)
    )
    qp.append(q_send(2, 0, 1, 1, yp))
    qm.append(q_send(3, 0, 3, 0, ym))

    m_ref[...] = jnp.full_like(m_ref, NEG)
    l_ref[...] = jnp.zeros_like(l_ref)
    acc[...] = jnp.zeros_like(acc)

    local[2].wait()

    def suffix(i, carry):
        for n in range(4):
            rows = pl.ds(pl.multiple_of(i * 128 + n * 32, 32), 32)
            toks = pl.ds(pl.multiple_of(i * 256 + n * 64, 64), 64)
            sc = dot(qbuf[0, rows, 0:576], s_in[toks, :], NT) * C2
            sc = jnp.where(lanes < len_ref[4 * i + n], sc, F32(NEG))
            top = jnp.max(sc, axis=1, keepdims=True)
            weight = jnp.exp2(sc - top)
            m_ref[rows, :] = jnp.broadcast_to(top, (32, 128))
            l_ref[rows, :] = jnp.broadcast_to(jnp.sum(weight, axis=1, keepdims=True), (32, 128))
            start = dot(weight.astype(BF16), s_in[toks, 0:512], NN)
            for j in range(4):
                acc[j, rows, :] = start[:, 128 * j : 128 * j + 128]
        return carry


    def score(s, r):
        return dot(qbuf[s], kbuf[r], NT)

    def fold(s, r, sc):
        rows = pl.ds(s * 256, 256)
        before = m_ref[rows, :]
        after = jnp.maximum(before, jnp.max(sc, axis=1, keepdims=True) * C2)
        shrink = jnp.exp2(before - after)
        weight = jnp.exp2(sc * C2 - after[:, :1])
        l_ref[rows, :] = l_ref[rows, :] * shrink + jnp.sum(weight, axis=1, keepdims=True)
        m_ref[rows, :] = after
        more = dot(weight.astype(BF16), kbuf[r, :, 0:512], NN)
        for j in range(4):
            acc[j, rows, :] = acc[j, rows, :] * shrink + more[:, 128 * j : 128 * j + 128]

    def attend(todo):
        now = score(*todo[0])
        for n, (s, r) in enumerate(todo):
            later = score(*todo[n + 1]) if n + 1 < len(todo) else None
            fold(s, r, now)
            now = later

    kx, kc = {}, {}

    def from_z(*parts):
        for piece in (0, 1):
            for r, xb in parts:
                kz[r, xb, piece].wait_recv()
                if r in (1, 2):
                    ring(r + 1, xb, piece, k_rows(r, xb, piece))
                elif r in (7, 6):
                    ring(r - 1, xb, piece, k_rows(r, xb, piece))
                elif (r, xb) in ((3, 0), (5, 1)):
                    ring(4, xb, piece, k_rows(r, xb, piece))
        for r, xb in parts:
            if xb == 0:
                half = kbuf.at[r, 0:64]
                kx[r] = (
                    send(half, kbuf.at[r, 128:192], kx_s.at[r, 0], kx_r.at[r, 0], same_x),
                    send(half, kbuf.at[r, 192:256], kx_s.at[r, 1], kx_r.at[r, 1], other_x),
                )
            else:
                kc[r] = [
                    send(kbuf.at[r, 0:128], kbuf.at[r, 256:384], kc_s.at[r, 0], kc_r.at[r, 0], sib)
                ]

    def from_x(r):
        for copy in kx[r]:
            copy.wait_recv()
        kc[r].append(
            send(kbuf.at[r, 128:256], kbuf.at[r, 384:512], kc_s.at[r, 1], kc_r.at[r, 1], sib)
        )

    def ready(r):
        for copy in kc[r]:
            copy.wait_recv()

    for piece in (0, 1):
        ox[piece].wait_recv()
        for r in (1, 7):
            ring(r, 1, piece, k_rows(0, 1, piece))
    from_z((1, 0), (7, 0))
    ox[2].wait_recv()
    sib0 = send(kbuf.at[0, 256:384], kbuf.at[0, 384:512], kc_s.at[0, 0], kc_r.at[0, 0], sib)
    qp[0].wait_recv()
    q2 = [q_send(4, 1, 2, 0, yp)]
    qm[0].wait_recv()
    q2.append(q_send(5, 3, 2, 1, ym))
    lax.fori_loop(0, 2, suffix, 0)
    from_z((1, 1), (7, 1))
    sib0.wait_recv()
    attend([(0, 0)])
    from_z((2, 0), (6, 0))
    from_x(1)
    from_x(7)
    qp[1].wait_recv()
    qm[1].wait_recv()
    attend([(1, 0), (3, 0)])
    from_z((2, 1), (6, 1))
    ready(1)
    ready(7)
    attend([(0, 1), (1, 1), (3, 1)])
    from_z((3, 0), (5, 0))
    from_x(2)
    from_x(6)
    attend([(0, 7), (1, 7), (3, 7)])
    for copy in q2:
        copy.wait_recv()
    from_z((3, 1), (5, 1))
    local[3].wait()
    ws = []
    for d in (2, 1, 3):
        to = (y + d) % 4
        cols = pl.ds(pl.multiple_of(1024 * to, 1024), 1024)
        ws.append(
            send(w_in.at[:, cols], wbuf.at[80 * d : 80 * d + 80], w_s.at[d], w_r.at[d], dev(y_=to))
        )
    attend([(2, 0), (2, 1), (2, 7)])
    from_z((4, 0))
    ready(2)
    ready(6)
    attend([(0, 2), (1, 2), (2, 2), (3, 2)])
    from_x(3)
    from_x(5)
    from_z((4, 1))
    attend([(0, 6), (1, 6), (2, 6), (3, 6)])
    ready(3)
    attend([(0, 3), (1, 3), (2, 3), (3, 3)])
    from_x(4)
    ready(5)
    attend([(0, 5), (1, 5), (2, 5), (3, 5)])
    ready(4)
    attend([(0, 4), (1, 4), (2, 4), (3, 4)])
    wbuf[0:80, :] = w_in[:, pl.ds(pl.multiple_of(1024 * y, 1024), 1024)]

    local[4].wait()

    heads_out = {}
    for half in (0, 1):
        heads_out[half] = []
        for d in (2, 1, 3, 0):
            to = (y + d) % 4
            for n in range(4):
                h = to * 8 + half * 4 + n
                parts, logs = [], []
                for a in range(4):
                    rows = pl.ds(((y + 4 - a) % 4) * 256 + h, 8, stride=32)
                    tot = l_ref[rows, :]
                    inv = 1.0 / tot
                    parts.append(
                        jnp.concatenate([acc[j, rows, :] * inv for j in range(4)], axis=1)
                    )
                    logs.append(m_ref[rows, :] + jnp.log2(tot))
                attn = jnp.concatenate(parts, axis=0).astype(BF16)
                hv_send[d, half, 32 * n : 32 * n + 32, :] = dot(attn, uv[h], NN).astype(BF16)
                lse_full[32 * n : 32 * n + 32, :] = jnp.concatenate(logs, axis=0)
            lse_send[d, half] = lse_full[...].T[0:8, :]
            if d:
                n = 2 * half
                who = dev(y_=to)
                heads_out[half] += [
                    send(hv_send.at[d, half], hv_recv.at[d, half], a_s.at[d, n], a_r.at[d, n], who),
                    send(
                        lse_send.at[d, half], lse_recv.at[d, half],
                        a_s.at[d, n + 1], a_r.at[d, n + 1], who,
                    ),
                ]

    hz, hx = {}, {}

    def along_z(r, half, start):
        steps = (r - start) % 8
        who = dev(z_=(z + steps) % 8)
        hz[r, half] = send(
            units.at[start, 0, half], units.at[r, 0, half],
            h_s.at[r, half], h_r.at[r, half], who,
        )

    def crossed_along_z(r, half, start):
        hx[r, half] = send(
            units.at[start, 1, half], units.at[r, 1, half],
            hx_s.at[r, half], hx_r.at[r, half], zp if r in (1, 3) else zm,
        )

    def cross(r, half):
        hx[r, half] = send(
            units.at[r, 0, half], units.at[r, 1, half], hx_s.at[r, half], hx_r.at[r, half], across
        )

    def place_unit(r, xb, half):
        base = (xh if xb == 0 else 1 - xh) * 256 + ((z + 8 - r) % 8) * 8
        unit = units[r, xb, half].astype(F32)
        for a in range(4):
            rows = pl.ds(pl.multiple_of(base + 64 * a, 8), 8)
            hv_all[rows, 512 * half : 512 * half + 512] = unit[8 * a : 8 * a + 8, :]

    for half in (0, 1):
        for copy in heads_out[half]:
            copy.wait_recv()
        logs = [lse_send[0, half]] + [lse_recv[d, half] for d in (1, 2, 3)]
        best = jnp.maximum(jnp.maximum(logs[0], logs[1]), jnp.maximum(logs[2], logs[3]))
        part = [jnp.exp2(x - best) for x in logs]
        norm = 1.0 / (part[0] + part[1] + part[2] + part[3])
        share = [jnp.concatenate([x * norm] * 16, axis=0).T for x in part]
        total = share[0] * hv_send[0, half].astype(F32)
        for d in (1, 2, 3):
            total = total + share[d] * hv_recv[d, half].astype(F32)
        total = total.astype(BF16)
        for h in range(4):
            units[0, 0, half, :, 128 * h : 128 * h + 128] = total[32 * h : 32 * h + 32, :]
        for r in (2, 6, 1, 7):
            along_z(r, half, 0)
        cross(0, half)
    place_unit(0, 0, 0)
    place_unit(0, 0, 1)
    def sums(n, d, dh, who):
        return pltpu.make_async_remote_copy(
            src_ref=out_send.at[dh, 80 * d : 80 * d + 80], dst_ref=rs.at[n],
            send_sem=rs_s.at[n], recv_sem=rs_r.at[n], device_id=who, device_id_type=MESH,
        )

    def project(to_p):
        dp = (p + to_p) % 2
        for dc in (1, 0):
            to_c = c if dc == 0 else 1 - c
            dh = 2 * dp + dc
            rows = pl.ds(pl.multiple_of(128 * (2 * to_p + to_c), 128), 128)
            out_send[dh] = dot(wbuf[...], hv_all[rows, :].astype(BF16), NT).astype(BF16)
            for d in (2, 1, 3):
                sums(4 * d + dh, d, dh, dev(y_=(y + 4 - d) % 4, p_=to_p, c_=to_c)).start()
            if dc:
                sums(dh, 0, dh, dev(p_=to_p, c_=to_c)).start()
            else:

                @pl.when(dp == 1)
                def _():
                    sums(2, 0, 2, dev(p_=1 - p)).start()

    done = 0
    while done < len(sent) and sent[done] is not hz[2, 0]:
        sent[done].wait_send()
        done += 1
    for half in (0, 1):
        for r in (1, 7, 2, 6):
            hz[r, half].wait_recv()
            if r == 2:
                along_z(3, half, 2)
                if half == 0:
                    along_z(4, half, 2)
            elif r == 6:
                along_z(5, half, 6)
                if half == 1:
                    along_z(4, half, 6)
            if r in (2, 6):
                cross(r, half)
    for half in (0, 1):
        hx[0, half].wait_recv()
        for r in (1, 7):
            crossed_along_z(r, half, 0)
    for r in (1, 7, 2, 6):
        for half in (0, 1):
            place_unit(r, 0, half)
    for half in (0, 1):
        place_unit(0, 1, half)
    for half in (0, 1):
        hx[2, half].wait_recv()
        crossed_along_z(3, half, 2)
        hx[6, half].wait_recv()
        crossed_along_z(5, half, 6)
        hz[4, half].wait_recv()
        cross(4, half)
        for r in (2, 6):
            place_unit(r, 1, half)
    for r, half in ((4, 0), (4, 1)):
        place_unit(r, 0, half)
    for r, half in ((3, 0), (5, 0), (3, 1), (5, 1)):
        hz[r, half].wait_recv()
        place_unit(r, 0, half)
    for copy in ws:
        copy.wait_recv()
    project(xh)
    for r, half in (
        (1, 0), (7, 0), (1, 1), (7, 1), (3, 0), (5, 0), (4, 0), (3, 1), (5, 1), (4, 1)
    ):
        hx[r, half].wait_recv()
        place_unit(r, 1, half)

    project(1 - xh)
    result = out_send[0, 0:80, :].astype(F32)
    back = [
        sums(4 * d + dh, d, dh, peer(d, dh)) for d in range(4) for dh in range(4) if d or dh
    ]
    for copy in sent[done:]:
        copy.wait_send()
    for copy in back:
        copy.wait_recv()
    for n in range(1, 16):
        result = result + rs[n].astype(F32)
    out_ref[...] = result.astype(BF16)
    for copy in back:
        copy.wait_send()


def per_device(
    queries, prefix_latent, suffix_latent, suffix_len, prefix_blocks, caption_reach, w_uv, w_out
):
    dma = pltpu.SemaphoreType.DMA
    return pl.pallas_call(
        kernel,
        out_shape=jax.ShapeDtypeStruct((80, 128), BF16),
        in_specs=[pl.BlockSpec(memory_space=pl.ANY)] * 5
        + [pl.BlockSpec(memory_space=pltpu.SMEM)] * 3,
        out_specs=pl.BlockSpec(memory_space=pltpu.VMEM),
        scratch_shapes=[
            pltpu.VMEM((256, 576), BF16),
            pltpu.VMEM((576, 256), BF16),
            pltpu.VMEM((512, 576), BF16),
            pltpu.VMEM((32, 512, 128), BF16),
            pltpu.VMEM((80, 4096), BF16),
            pltpu.VMEM((4, 256, 640), BF16),
            pltpu.VMEM((8, 512, 640), BF16),
            pltpu.VMEM((4, 1024, 128), F32),
            pltpu.VMEM((1024, 128), F32),
            pltpu.VMEM((1024, 128), F32),
            pltpu.VMEM((320, 1024), BF16),
            pltpu.VMEM((4, 2, 128, 128), BF16),
            pltpu.VMEM((128, 128), F32),
            pltpu.VMEM((4, 2, 8, 128), F32),
            pltpu.VMEM((4, 2, 128, 128), BF16),
            pltpu.VMEM((4, 2, 8, 128), F32),
            pltpu.VMEM((8, 2, 2, 32, 512), BF16),
            pltpu.VMEM((512, 1024), F32),
            pltpu.VMEM((4, 320, 128), BF16),
            pltpu.VMEM((16, 80, 128), BF16),
            dma((5,)),
            dma((8, 4)), dma((8, 4)),
            dma((8, 3)), dma((8, 3)),
            dma((8, 2)), dma((8, 2)),
            dma((6,)), dma((6,)),
            dma((4,)), dma((4,)),
            dma((4, 4)), dma((4, 4)),
            dma((8, 2)), dma((8, 2)),
            dma((8, 2)), dma((8, 2)),
            dma((16,)), dma((16,)),
        ],
        compiler_params=pltpu.CompilerParams(
            collective_id=0, has_side_effects=True, vmem_limit_bytes=56 * 2**20
        ),
    )(
        queries.reshape(256, 576),
        prefix_latent.T,
        suffix_latent.reshape(512, 576),
        w_uv,
        w_out.T,
        suffix_len,
        prefix_blocks,
        caption_reach,
    ).T


def solution(mesh):
    placed = (
        P("blk", "heads", None),
        P("blk", None),
        P("blk", None, None),
        P("blk"),
        P(),
        P("blk"),
        P("heads", None, None),
        P("heads", "blk"),
    )
    return jax.shard_map(
        per_device, mesh=mesh, in_specs=placed, out_specs=P("heads", "blk"), check_vma=False
    )
```
